256 devices in a mesh: blk: 16 (over z, y_hi), img: 16 (over x, y_lo, core).
Axes of the slice: x: 4, y: 4 (y_hi: 2, y_lo: 2; y = y_hi * 2 + y_lo), z: 8, core: 2. Of those that a mesh axis runs over, the one named last changes fastest.
Arguments:
- features: bfloat16 [16384, 768], P(('blk', 'img')), may hold values from -6 to 6
- proj: bfloat16 [768, 768], replicated, may hold values from -0.21875 to 0.21875
- student_text: bfloat16 [16384, 768], P(('blk', 'img')), may hold values from -6 to 6
- teacher_image: bfloat16 [16384, 1024], P(('blk', 'img')), may hold values from -25 to 25
- teacher_text: bfloat16 [16384, 1024], P(('blk', 'img')), may hold values from -5 to 5
Outputs:
- row_loss: float32 [16384], P(('blk', 'img'))
- loss: float32 [], replicated
- grad_proj: float32 [768, 768], P('img')
The draws below stay inside these ranges and needn't reach their ends.
All inputs are finite; a program needn't handle non-finite values.
Results may differ from the reference program's by a relative error of at most 0.003.
Values may be sent and summed in bfloat16 or wider, within the bound.
No kernel may reach another device: no remote copies, remote signals or barrier semaphores. Data moves between devices by JAX's collectives and lax.ppermute only.
A program may use at most 64 MiB of HBM per device.

```python
import jax
import jax.numpy as jnp
from jax import lax

FEAT = 768
D_S = 768
D_T = 1024
ROWS_DEV = 64
BATCH = 16384
N_BLK = 16
N_IMG = 16


def teacher_pair(key):
    text = jax.random.truncated_normal(jax.random.fold_in(key, 11), -5.0, 5.0, (BATCH, D_T), jnp.float32)
    image = jax.random.truncated_normal(jax.random.fold_in(key, 12), -5.0, 5.0, (BATCH, D_T), jnp.float32)
    return (text, image)


def draw_teacher_text(key, part):
    text, image = teacher_pair(key)
    return text.astype(jnp.bfloat16)


def draw_teacher_image(key, part):
    text, image = teacher_pair(key)
    return image.astype(jnp.bfloat16)


def steps_of(key, shape, pieces, smallest, high):
    def one(dim, shards_of):
        draws = jax.random.uniform(jax.random.fold_in(jax.random.fold_in(key, 6), dim), (shards_of,), jnp.float32, smallest / len(pieces), high / len(pieces))
        return jnp.repeat(jnp.exp(draws), shape[dim] // shards_of).reshape((-1,) + (1,) * (len(shape) - dim - 1))

    level = one(*pieces[0])
    for cut in pieces[1:]:
        level = level * one(*cut)
    return level


def scatter_about(own_key, shape, deviation, reach, shards=(), kind=jnp.bfloat16):
    values = deviation * jax.random.normal(own_key, shape, jnp.float32)
    if shards:
        values = values * steps_of(own_key, shape, shards, -0.22, 0.18)
    return jnp.clip(values, -reach, reach).astype(kind)


def setup_inputs(seed: int = 0) -> dict:
    keys = jax.random.split(jax.random.key(seed), 6)
    features = scatter_about(keys[0], (BATCH, FEAT), 1.0, 6.0, ((0, 256),))
    proj = scatter_about(keys[1], (FEAT, D_S), FEAT ** -0.5, 0.21875)
    student_text = scatter_about(keys[2], (BATCH, D_S), 1.0, 6.0, ((0, 256),))
    teacher_image = draw_teacher_image(jax.random.fold_in(keys[5], 71), 0)
    teacher_text = draw_teacher_text(jax.random.fold_in(keys[5], 71), 0)
    return {"features": features, "proj": proj, "student_text": student_text, "teacher_image": teacher_image, "teacher_text": teacher_text}


sig_scale = 10.0
sig_bias = -10.0
teacher_gain = 3.0
eps_value = 1e-06

def unit_rows(values):
    norms = jnp.sqrt(lax.optimization_barrier(jnp.sum(values * values, axis=-1, keepdims=True)) + eps_value)
    return (values / norms, norms)

def reference(features, proj, student_text, teacher_image, teacher_text):
    pre = jnp.dot(features, proj, preferred_element_type=jnp.float32)
    s_img, norms = unit_rows(pre)
    s_img_b = s_img.astype(jnp.bfloat16)
    s_txt, unused = unit_rows(student_text.astype(jnp.float32))
    s_txt_b = s_txt.astype(jnp.bfloat16)
    block = ROWS_DEV * N_IMG
    gain = teacher_gain / jnp.sqrt(jnp.float32(D_T))

    def rows_of(index):
        start = (index * block).astype(jnp.int32)
        image_b = lax.dynamic_slice_in_dim(s_img_b, start, block, 0)
        t_image = lax.dynamic_slice_in_dim(teacher_image, start, block, 0)
        cosine = jnp.dot(image_b, s_txt_b.T, preferred_element_type=jnp.float32)
        t_logit = gain * jnp.dot(t_image, teacher_text.T, preferred_element_type=jnp.float32)
        s_logit = sig_scale * cosine
        t_max = lax.optimization_barrier(jnp.max(t_logit, axis=1, keepdims=True))
        t_exp = jnp.exp(t_logit - t_max)
        t_sum = lax.optimization_barrier(jnp.sum(t_exp, axis=1, keepdims=True))
        t_prob = t_exp / t_sum
        s_exp = jnp.exp(s_logit)
        s_sum = lax.optimization_barrier(jnp.sum(s_exp, axis=1, keepdims=True))
        s_prob = s_exp / s_sum
        row_ids = start + jnp.arange(block, dtype=jnp.int32)[:, None]
        col_ids = jnp.arange(BATCH, dtype=jnp.int32)[None, :]
        sign = jnp.where(row_ids == col_ids, jnp.float32(1.0), jnp.float32(-1.0))
        margin = s_logit + sig_bias
        terms = lax.optimization_barrier(jnp.sum(t_prob * (t_logit - s_logit) + jax.nn.softplus(-sign * margin), axis=1))
        row_part = terms - (t_max[:, 0] + jnp.log(t_sum[:, 0])) + jnp.log(s_sum[:, 0])
        d_cos = (sig_scale * (s_prob - t_prob) - sig_scale * sign * jax.nn.sigmoid(-sign * margin)).astype(jnp.bfloat16)
        d_part = jnp.dot(d_cos, s_txt_b, preferred_element_type=jnp.float32)
        return (row_part, d_part)
    row_blocks, d_blocks = lax.map(rows_of, jnp.arange(N_BLK, dtype=jnp.int32))
    row_loss = row_blocks.reshape(BATCH)
    d_simg = d_blocks.reshape(BATCH, D_S)
    along = lax.optimization_barrier(jnp.sum(s_img * d_simg, axis=1, keepdims=True))
    d_pre = (d_simg - s_img * along) / norms
    grad_proj = jnp.dot(features.astype(jnp.float32).T, d_pre, precision=lax.Precision.HIGHEST)
    loss = jnp.sum(row_loss) / BATCH
    return (row_loss, loss, grad_proj)
```

```python
import functools

import jax
import jax.numpy as jnp
import numpy as np
from jax import lax
from jax.experimental import pallas as pl
from jax.experimental.pallas import tpu as pltpu
from jax.sharding import Mesh, PartitionSpec as P

sig_scale = 10.0
sig_bias = -10.0
teacher_gain = 3.0
eps_value = 1e-06

F32 = jnp.float32
BF16 = jnp.bfloat16
NT = (((1,), (1,)), ((), ()))
ALL = ("z", "yh", "x", "yl", "c")
Y = ("yh", "yl")
VMEM_LIMIT = 56 * 1024 * 1024
COLS = 256
CHUNK = 128


def ring(n, k):
    return [(i, (i + k) % n) for i in range(n)]


def flip(n, k):
    return [(i, i ^ k) for i in range(n)]


def whole(shape):
    return pl.BlockSpec(shape, lambda i: (0,) * len(shape))


def logits_kernel(gain, pair_ref, ttxt_ref, stxt_ref, projt_ref, self_ref,
                  te_ref, se_ref, sig_ref, simg_ref, stats_ref, tl, sl):
    dt = ttxt_ref.shape[1]
    texts = ttxt_ref.shape[0]
    tl[...] = gain * lax.dot_general(ttxt_ref[...], pair_ref[:, :dt], NT, preferred_element_type=F32)
    pre = lax.dot_general(projt_ref[...], pair_ref[:, dt:], NT, preferred_element_type=F32)
    norm = jnp.sqrt(jnp.sum(pre * pre, axis=0, keepdims=True) + eps_value)
    simg = pre / norm
    simg_ref[...] = simg
    sl[...] = sig_scale * jnp.dot(stxt_ref[...], simg.astype(BF16), preferred_element_type=F32)
    t_max = jnp.max(tl[...], axis=0, keepdims=True)
    shrink = float(np.exp(sig_bias))

    def step(k, sums):
        rows = pl.ds(pl.multiple_of(k * CHUNK, CHUNK), CHUNK)
        t = tl[rows, :]
        s = sl[rows, :]
        te = jnp.exp(t - t_max)
        se = jnp.exp(s)
        em = se * shrink
        up = 1.0 + em
        inv = 1.0 / up
        sig = em * inv
        soft = jnp.log(up) + (em - (up - 1.0)) * inv
        te_ref[rows, :] = te.astype(BF16)
        se_ref[rows, :] = se.astype(BF16)
        sig_ref[rows, :] = sig.astype(BF16)
        terms = (te, se, te * (t - s), soft)
        return tuple(a + jnp.sum(v.reshape(CHUNK // 8, 8, v.shape[1]), axis=0) for a, v in zip(sums, terms))

    zero = jnp.zeros((8, tl.shape[1]), F32)
    sums = lax.fori_loop(0, texts // CHUNK, step, (zero,) * 4)
    rows = [t_max] + [jnp.sum(v, axis=0, keepdims=True) for v in sums] + [norm]
    rows[4] = rows[4] + self_ref[...]
    stats_ref[...] = jnp.concatenate(rows + [jnp.zeros((2, tl.shape[1]), F32)], axis=0)


def embed_kernel(te_ref, se_ref, sig_ref, simg_ref, stats_ref, txtt_ref, pair_ref, a_ref, b_ref, c_ref, ft_ref):
    simg = simg_ref[...]
    inv = 1.0 / stats_ref[5:6, :]
    for src, dst in ((se_ref, a_ref), (te_ref, b_ref), (sig_ref, c_ref)):
        d = jnp.dot(txtt_ref[...], src[...], preferred_element_type=F32)
        along = jnp.sum(simg * d, axis=0, keepdims=True)
        dst[...] = (d - simg * along) * inv
    width = pair_ref.shape[1] - ft_ref.shape[0]
    ft_ref[...] = pair_ref[:, width:].T


def away_kernel(coef_ref, a_ref, b_ref, c_ref, ft_ref, diag_ref, d_ref, out_ref, acc):
    d = coef_ref[0:1, :] * a_ref[...] + coef_ref[1:2, :] * b_ref[...] + sig_scale * c_ref[...]
    d = d.astype(BF16)
    d_ref[...] = d

    @pl.when(pl.program_id(0) == 0)
    def _():
        acc[...] = diag_ref[...]

    acc[...] += lax.dot_general(ft_ref[...], d, NT, preferred_element_type=F32)

    @pl.when(pl.program_id(0) == pl.num_programs(0) - 1)
    def _():
        out_ref[...] = acc[...].astype(BF16)


def home_kernel(ft_ref, d_ref, diag_ref, out_ref):
    out_ref[...] = diag_ref[...] + lax.dot_general(ft_ref[...], d_ref[...], NT, preferred_element_type=F32)


def params():
    return pltpu.CompilerParams(vmem_limit_bytes=VMEM_LIMIT)


def merge(parts):
    top = functools.reduce(jnp.maximum, [p[0] for p in parts])
    tsum = 0.0
    ssum = 0.0
    tval = 0.0
    soft = 0.0
    for p in parts:
        w = jnp.exp(p[0] - top)
        tsum = tsum + w * p[1]
        ssum = ssum + p[2]
        tval = tval + w * p[3]
        soft = soft + p[4]
    return jnp.stack([top, tsum, ssum, tval, soft])


def per_device(features, proj, student_text, teacher_image, teacher_text):
    rows, feat = features.shape
    dt = teacher_text.shape[1]
    ds = student_text.shape[1]
    zi, yi, xi, ci = lax.axis_index("z"), lax.axis_index(Y), lax.axis_index("x"), lax.axis_index("c")
    yl = lax.axis_index("yl")
    zn, yn, xn = lax.axis_size("z"), lax.axis_size(Y), lax.axis_size("x")
    ylno = lax.axis_size("yl")
    batch = rows * zn * yn * xn * 2
    images = rows * yn * xn
    texts = rows * zn * 2
    gain = float(teacher_gain / np.sqrt(np.float32(dt)))
    cut = feat // (xn * ylno * 2)
    half = feat // 2

    ttxt = lax.all_gather(teacher_text, ("z", "c"), axis=0, tiled=True)
    st = student_text.astype(F32)
    st_own = (st / jnp.sqrt(jnp.sum(st * st, axis=-1, keepdims=True) + eps_value)).astype(BF16)
    stxt = lax.all_gather(st_own, ("z", "c"), axis=0, tiled=True)

    def by_core(v, axis):
        shape = v.shape[:axis] + (feat // (2 * cut), 2, cut) + v.shape[axis + 1:]
        v = v.reshape(shape)
        mine = lax.dynamic_index_in_dim(v, ci, axis + 1, keepdims=False)
        other = lax.dynamic_index_in_dim(v, 1 - ci, axis + 1, keepdims=False)
        out = jnp.concatenate([mine, other], axis=axis)
        return out.reshape(v.shape[:axis] + (feat,) + v.shape[axis + 3:])

    feats = by_core(features, 1)
    projt = by_core(proj, 0).T
    pair = jnp.concatenate([teacher_image, feats], axis=1)
    width = dt + feat

    column = jnp.zeros((yn, rows, width), BF16)
    got = [pair] + [lax.ppermute(pair, Y, ring(yn, k)) for k in (1, 3)]
    got.append(lax.ppermute(got[1], Y, ring(yn, 1)))
    for piece, back in zip(got, (0, 1, 3, 2)):
        column = lax.dynamic_update_slice(column, piece[None], (lax.rem(yi - back + yn, yn), 0, 0))
    column = column.reshape(yn * rows, width)
    from_left = lax.ppermute(column, "x", ring(xn, 1))
    from_right = lax.ppermute(column, "x", ring(xn, 3))
    mid = yn * rows // 2
    far_a = lax.ppermute(from_left[:mid], "x", ring(xn, 1))
    far_b = lax.ppermute(from_right[mid:], "x", ring(xn, 3))
    pairs = jnp.zeros((xn, yn * rows, width), BF16)
    for piece, back, start in ((column, 0, 0), (from_left, 1, 0), (from_right, 3, 0), (far_a, 2, 0), (far_b, 2, mid)):
        pairs = lax.dynamic_update_slice(pairs, piece[None], (lax.rem(xi - back + xn, xn), start, 0))
    pairs = pairs.reshape(images, width)

    pre = jnp.dot(feats, projt.T, preferred_element_type=F32)
    n_own = jnp.sqrt(jnp.sum(pre * pre, axis=-1, keepdims=True) + eps_value)
    s_own = pre / n_own
    s_diag = sig_scale * jnp.sum(s_own.astype(BF16).astype(F32) * st_own.astype(F32), axis=-1)
    self_row = lax.dynamic_update_slice(jnp.zeros((1, images), F32), -(s_diag + sig_bias)[None], (0, (xi * yn + yi) * rows))
    d_diag = -sig_scale * st_own.astype(F32)
    d_diag = (d_diag - s_own * jnp.sum(s_own * d_diag, axis=1, keepdims=True)) / n_own
    g_diag = jnp.dot(feats.astype(F32).T, d_diag, precision=lax.Precision.HIGHEST)

    blocks = images // COLS
    col = lambda n: pl.BlockSpec((n, COLS), lambda i: (0, i))
    te, se, sig, simg, stats = pl.pallas_call(
        functools.partial(logits_kernel, gain),
        grid=(blocks,),
        in_specs=[pl.BlockSpec((COLS, width), lambda i: (i, 0)), whole((texts, dt)), whole((texts, ds)), whole((ds, feat)), col(1)],
        out_specs=[col(texts), col(texts), col(texts), col(ds), col(8)],
        out_shape=[jax.ShapeDtypeStruct((texts, images), BF16)] * 3
        + [jax.ShapeDtypeStruct((ds, images), F32), jax.ShapeDtypeStruct((8, images), F32)],
        scratch_shapes=[pltpu.VMEM((texts, COLS), F32), pltpu.VMEM((texts, COLS), F32)],
        compiler_params=params(),
        cost_estimate=pl.CostEstimate(flops=2 * images * (texts * (dt + ds) + feat * ds), bytes_accessed=20 << 20, transcendentals=4 * images * texts),
        name="logits",
    )(pairs, ttxt, stxt, projt, self_row)

    a, b, c, ft = pl.pallas_call(
        embed_kernel,
        grid=(blocks,),
        in_specs=[col(texts), col(texts), col(texts), col(ds), col(8), whole((ds, texts)), pl.BlockSpec((COLS, width), lambda i: (i, 0))],
        out_specs=[col(ds), col(ds), col(ds), col(feat)],
        out_shape=[jax.ShapeDtypeStruct((ds, images), F32)] * 3 + [jax.ShapeDtypeStruct((feat, images), BF16)],
        compiler_params=params(),
        cost_estimate=pl.CostEstimate(flops=6 * images * texts * ds, bytes_accessed=20 << 20, transcendentals=0),
        name="embed",
    )(te, se, sig, simg, stats, stxt.T, pairs)

    own = stats[:5]
    own = merge([own] + [lax.ppermute(own, Y, ring(yn, k)) for k in (1, 3, 2)])
    own = merge([own] + [lax.ppermute(own, "x", ring(xn, k)) for k in (1, 3, 2)])
    t_max, t_sum, s_sum, t_val, soft = own
    coef = jnp.stack([sig_scale / s_sum, -sig_scale * jnp.exp(stats[0] - t_max) / t_sum])

    d, away = pl.pallas_call(
        away_kernel,
        grid=(blocks,),
        in_specs=[col(2), col(ds), col(ds), col(ds), pl.BlockSpec((half, COLS), lambda i: (1, i)), pl.BlockSpec((half, ds), lambda i: (1, 0))],
        out_specs=[col(ds), whole((half, ds))],
        out_shape=[jax.ShapeDtypeStruct((ds, images), BF16), jax.ShapeDtypeStruct((half, ds), BF16)],
        scratch_shapes=[pltpu.VMEM((half, ds), F32)],
        compiler_params=params(),
        name="away",
    )(coef, a, b, c, ft, g_diag)
    arrived = lax.ppermute(away, "c", flip(2, 1))
    home = pl.pallas_call(
        home_kernel,
        grid=(1,),
        in_specs=[pl.BlockSpec((half, images), lambda i: (0, 0)), whole((ds, images)), pl.BlockSpec((half, ds), lambda i: (0, 0))],
        out_specs=whole((half, ds)),
        out_shape=jax.ShapeDtypeStruct((half, ds), F32),
        compiler_params=params(),
        cost_estimate=pl.CostEstimate(flops=2 * images * half * ds, bytes_accessed=6 << 20, transcendentals=0),
        name="home",
    )(ft, d, g_diag)

    value = t_val / t_sum + soft - (t_max + jnp.log(t_sum)) + jnp.log(s_sum)
    row_loss = lax.dynamic_slice_in_dim(value, (xi * yn + yi) * rows, rows, 0)
    loss_row = jnp.full((8, 128), jnp.sum(value), F32)
    loss_row = loss_row + lax.ppermute(loss_row, "c", flip(2, 1))

    g = (home + arrived.astype(F32)).reshape(xn, ylno * cut, ds)
    send = lambda k: lax.ppermute(lax.dynamic_index_in_dim(g, lax.rem(xi + k, xn), 0, keepdims=False).astype(BF16), "x", ring(xn, k))
    parts = [send(k) for k in (1, 3, 2)]
    g = lax.dynamic_index_in_dim(g, xi, 0, keepdims=False) + sum(p.astype(F32) for p in parts)
    g = g.reshape(ylno, cut, ds)
    mine = lax.dynamic_index_in_dim(g, yl, 0, keepdims=False)
    other = lax.dynamic_index_in_dim(g, 1 - yl, 0, keepdims=False).astype(BF16)
    parts = [lax.ppermute(other, Y, ring(yn, k)) for k in (1, 3)] + [lax.ppermute(mine.astype(BF16), Y, ring(yn, 2))]
    mine = mine + sum(p.astype(F32) for p in parts)
    tail = jnp.concatenate([mine, jnp.broadcast_to(loss_row[:, :1], (8, ds))], axis=0)
    for k in (1, 2, 4):
        tail = tail + lax.ppermute(tail, "z", flip(zn, k))
    return (row_loss, tail[cut, 0] / batch, tail[:cut])


def solution(mesh):
    sizes = dict(mesh.shape)
    fine = Mesh(np.asarray(mesh.devices).reshape(sizes["blk"] // 2, 2, sizes["img"] // 4, 2, 2), ALL)
    return jax.shard_map(
        per_device,
        mesh=fine,
        in_specs=(P(ALL, None), P(), P(ALL, None), P(ALL, None), P(ALL, None)),
        out_specs=(P(ALL), P(), P(("x", "yl", "c"), None)),
        check_vma=False,
    )
```

```python
import functools

import jax
import jax.numpy as jnp
import numpy as np
from jax import lax
from jax.experimental import pallas as pl
from jax.experimental.pallas import tpu as pltpu
from jax.sharding import Mesh, PartitionSpec as P

sig_scale = 10.0
sig_bias = -10.0
teacher_gain = 3.0
eps_value = 1e-06

F32 = jnp.float32
BF16 = jnp.bfloat16
LOG2E = float(np.log2(np.e))
LN2 = float(np.log(2.0))
NT = (((1,), (1,)), ((), ()))
ALL = ("z", "yh", "x", "yl", "c")
Y = ("yh", "yl")
VMEM_LIMIT = 48 * 1024 * 1024
LANES = 128
STEP = 32


def ring(n, k):
    return [(i, (i + k) % n) for i in range(n)]


def flip(n, k):
    return [(i, i ^ k) for i in range(n)]


SMEM = pl.BlockSpec(memory_space=pltpu.SMEM)
VMEM = pl.BlockSpec(memory_space=pltpu.VMEM)


def shape(dims, dtype):
    return jax.ShapeDtypeStruct(dims, dtype)


def params():
    return pltpu.CompilerParams(vmem_limit_bytes=VMEM_LIMIT)


def cost(macs, megabytes, exps=0):
    return pl.CostEstimate(flops=int(2 * macs), bytes_accessed=int(megabytes * 1e6), transcendentals=int(exps))


def images_kernel(zn, dt, place_ref, own_txt_ref, proj_ref, *refs):
    pieces, (timg_ref, feat_ref, simg_ref, simgb_ref, inv_ref, self_ref, diag_ref) = refs[:zn], refs[zn:]
    rows = pieces[0].shape[0]
    z = place_ref[0]
    for k, piece in enumerate(pieces):
        at = pl.ds(pl.multiple_of(lax.rem(z + zn - k, zn) * rows, rows), rows)
        timg_ref[at, :] = piece[:, :dt]
        feat_ref[at, :] = piece[:, dt:]
    pre = jnp.dot(feat_ref[...], proj_ref[...], preferred_element_type=F32)
    norm = jnp.sqrt(jnp.sum(pre * pre, axis=1, keepdims=True) + eps_value)
    simg = pre / norm
    simg_ref[...] = simg
    simgb_ref[...] = simg.astype(BF16)
    inv_ref[...] = jnp.broadcast_to(1.0 / norm, inv_ref.shape)
    own = pl.ds(pl.multiple_of(z * rows, rows), rows)
    s = simg_ref[own, :]
    txt = own_txt_ref[...].astype(F32)
    margin = sig_scale * jnp.sum(s.astype(BF16).astype(F32) * txt, axis=1, keepdims=True) + sig_bias
    self_ref[...] = jnp.zeros_like(self_ref)
    self_ref[own, :] = jnp.broadcast_to(-margin, (rows, LANES))
    d = -sig_scale * txt
    diag_ref[...] = (d - s * jnp.sum(s * d, axis=1, keepdims=True)) * inv_ref[own, 0:1]


def make_block(first, gain, sizes):
    def kernel(timg_ref, simgb_ref, old_ref, *refs):
        texts, refs = refs[:len(sizes)], refs[len(sizes):]
        if not first:
            refs = refs[4:]
        te_ref, se_ref, sig_ref, stu_ref, stat_ref, flat_ref, tl, sl = refs
        dt = timg_ref.shape[1]
        at = 0
        for ref, n in zip(texts, sizes):
            tl[:, at:at + n] = lax.dot_general(timg_ref[...], ref[:, :dt], NT, preferred_element_type=F32)
            sl[:, at:at + n] = lax.dot_general(simgb_ref[...], ref[:, dt:], NT, preferred_element_type=F32)
            stu_ref[at:at + n, :] = ref[:, dt:]
            at += n
        lane = lax.broadcasted_iota(jnp.int32, (STEP, LANES), 1)
        shrink = float(np.exp(sig_bias))
        for r in range(0, timg_ref.shape[0], STEP):
            rows = slice(r, r + STEP)
            t = (gain * LOG2E) * tl[rows, :]
            s = (sig_scale * LOG2E) * sl[rows, :]
            old = old_ref[rows, :]
            top = jnp.max(t, axis=1, keepdims=True)
            if not first:
                top = jnp.maximum(top, old[:, 0:1])
            te = jnp.exp2(t - top)
            se = jnp.exp2(s)
            em = se * shrink
            up = 1.0 + em
            sig = em * pl.reciprocal(up, approx=True)
            soft = jnp.log(up) + (em - (up - 1.0))
            te_ref[rows, :] = te.astype(BF16)
            se_ref[rows, :] = se.astype(BF16)
            sig_ref[rows, :] = sig.astype(BF16)
            total = lambda v: jnp.sum(v, axis=1, keepdims=True)
            sums = [total(te), total(se), total(te * (t - s)), total(soft)]
            if first:
                sums[3] = sums[3] + old[:, 0:1]
            else:
                w = jnp.exp2(old[:, 0:1] - top)
                sums = [sums[0] + w * old[:, 1:2], sums[1] + old[:, 2:3], sums[2] + w * old[:, 3:4], sums[3] + old[:, 4:5]]
            stat = jnp.broadcast_to(top, (STEP, LANES))
            for n, v in enumerate(sums):
                stat = jnp.where(lane == n + 1, v, stat)
            stat_ref[rows, :] = stat
        flat_ref[...] = stat_ref[...].T[:8, :]

    return kernel


def embed_kernel(blocks, te_ref, se_ref, sig_ref, stu_ref, simg_ref, inv_ref, feat_ref, *refs):
    stats, (a_ref, b_ref, c_ref, ft_ref, scaled) = refs[:blocks], refs[blocks:]
    span = te_ref.shape[1] // blocks
    top = stats[-1][:, 0:1]
    for n in range(blocks):
        cols = slice(n * span, (n + 1) * span)
        w = jnp.exp2(stats[n][:, 0:1] - top)
        scaled[:, cols] = (te_ref[:, cols].astype(F32) * w).astype(BF16)
    simg = simg_ref[...]
    inv = inv_ref[:, 0:1]
    for src, dst in ((sig_ref, c_ref), (se_ref, a_ref), (scaled, b_ref)):
        d = jnp.dot(src[...], stu_ref[...], preferred_element_type=F32)
        along = jnp.sum(simg * d, axis=1, keepdims=True)
        dst[...] = ((d - simg * along) * inv).astype(BF16)
    ft_ref[...] = feat_ref[...].T


def away_kernel(place_ref, sums_ref, flat_ref, a_ref, b_ref, c_ref, diag_ref, ft_ref,
                out_ref, hi_ref, lo_ref, val_ref, turned, grad, cut_ft):
    rows = diag_ref.shape[0]
    half, ds = grad.shape[0], a_ref.shape[1]
    top, tsum, ssum, tval, soft = (sums_ref[k:k + 1, :] for k in range(5))
    value = tval / tsum * LN2 + soft - (top * LN2 + jnp.log(tsum)) + jnp.log(ssum)
    val_ref[...] = jnp.broadcast_to(value, val_ref.shape)
    ca = sig_scale / ssum
    cb = -sig_scale * jnp.exp2(flat_ref[0:1, :] - top) / tsum
    row = lax.broadcasted_iota(jnp.int32, (LANES, ca.shape[1]), 0)
    turned[...] = jnp.where(row == 0, ca, cb).T
    d = turned[:, 0:1] * a_ref[...].astype(F32) + turned[:, 1:2] * b_ref[...].astype(F32) + sig_scale * c_ref[...].astype(F32)
    images = d.shape[0]
    grad_d = d
    hi_ref[...] = grad_d.astype(BF16)
    lo_ref[...] = (grad_d - hi_ref[...].astype(F32)).astype(BF16)
    own = pl.ds(pl.multiple_of(place_ref[0] * rows, rows), rows)
    mine = hi_ref[own, :].astype(F32) + lo_ref[own, :].astype(F32) + diag_ref[...]
    mine_hi = mine.astype(BF16)
    hi_ref[own, :] = mine_hi
    lo_ref[own, :] = (mine - mine_hi.astype(F32)).astype(BF16)
    pick(cut_ft, ft_ref, 1 - place_ref[1])
    g = jnp.dot(cut_ft[...], hi_ref[...], preferred_element_type=F32)
    g = g + jnp.dot(cut_ft[...], lo_ref[...], preferred_element_type=F32)
    out_ref[:half, :] = g
    out_ref[half:, :] = jnp.broadcast_to(jnp.sum(value, axis=1, keepdims=True), (8, ds))


def pick(dst, src, core):
    groups = 8
    cut = dst.shape[0] // groups
    for g in range(groups):
        dst[g * cut:(g + 1) * cut, :] = src[pl.ds(pl.multiple_of((2 * g + core) * cut, cut), cut), :]


def home_kernel(place_ref, ft_ref, hi_ref, lo_ref, out_ref, cut_ft):
    pick(cut_ft, ft_ref, place_ref[1])
    out_ref[...] = jnp.dot(cut_ft[...], hi_ref[...], preferred_element_type=F32) + jnp.dot(
        cut_ft[...], lo_ref[...], preferred_element_type=F32)


def cores_kernel(xn, place_ref, home_ref, got_ref, away_ref, keep_ref, *sends):
    half = home_ref.shape[0]
    cut = half // xn
    loss = got_ref[half:, :] + away_ref[...]
    x = place_ref[2]
    at = pl.ds(pl.multiple_of(x * cut, cut), cut)
    keep_ref[:cut, :] = home_ref[at, :] + got_ref[at, :]
    keep_ref[cut:, :] = loss
    hi = loss.astype(BF16).astype(F32)
    mid = (loss - hi).astype(BF16).astype(F32)
    low = loss - hi - mid
    row = lax.broadcasted_iota(jnp.int32, loss.shape, 0)
    packed = jnp.where(row == 0, hi, jnp.where(row == 1, mid, jnp.where(row == 2, low, 0.0)))
    packed = jnp.concatenate([packed, jnp.zeros_like(packed)], axis=0).astype(BF16)
    for k, ref in zip((1, 3, 2), sends):
        at = pl.ds(pl.multiple_of(lax.rem(x + k, xn) * cut, cut), cut)
        ref[:cut, :] = (home_ref[at, :] + got_ref[at, :]).astype(BF16)
        ref[cut:, :] = packed


def rows_kernel(place_ref, keep_ref, p_ref, q_ref, r_ref, mine_ref, other_ref, total):
    cut = keep_ref.shape[0] - 8
    half = cut // 2
    total[...] = keep_ref[:cut, :]
    loss = keep_ref[cut:, :]
    for ref in (p_ref, q_ref, r_ref):
        total[...] += ref[:cut, :].astype(F32)
        packed = ref[cut:, :].astype(F32)
        loss = loss + (packed[0:1, :] + packed[1:2, :] + packed[2:3, :])
    y = place_ref[3]
    for ref, at in ((mine_ref, y), (other_ref, 1 - y)):
        ref[:half, :] = total[pl.ds(pl.multiple_of(at * half, half), half), :]
        ref[half:, :] = loss


def merge(*parts):
    top = functools.reduce(jnp.maximum, [p[0] for p in parts])
    out = [0.0] * 4
    for p in parts:
        w = jnp.exp2(p[0] - top)
        out = [out[0] + w * p[1], out[1] + p[2], out[2] + w * p[3], out[3] + p[4]]
    return jnp.stack([top] + out)


def per_device(features, proj, student_text, teacher_image, teacher_text):
    rows, feat = features.shape
    dt = teacher_text.shape[1]
    ds = student_text.shape[1]
    zn, yn, xn, cn = (lax.axis_size(a) for a in ("z", Y, "x", "c"))
    images = rows * zn
    batch = images * yn * xn * cn
    texts = rows * yn * xn * cn
    column = rows * yn
    gain = float(teacher_gain / np.sqrt(np.float32(dt)))
    half = feat // cn
    place = jnp.stack([lax.axis_index(a) for a in ("z", "c", "x", "yl")]).astype(jnp.int32)

    img = jnp.concatenate([teacher_image, features], axis=1)
    st = student_text.astype(F32)
    st_own = (st / jnp.sqrt(jnp.sum(st * st, axis=-1, keepdims=True) + eps_value)).astype(BF16)
    txt = jnp.concatenate([teacher_text, st_own], axis=1)

    up, down = [img], [img]
    for _ in range(zn // 2):
        up.append(lax.ppermute(up[-1], "z", ring(zn, 1)))
    for _ in range(zn // 2 - 1):
        down.append(lax.ppermute(down[-1], "z", ring(zn, zn - 1)))
    pieces = up + down[:0:-1]

    swap = lambda v: lax.ppermute(v, "c", flip(cn, 1))
    left = lax.ppermute(txt, Y, ring(yn, 1))
    right = lax.ppermute(txt, Y, ring(yn, yn - 1))
    far = lax.ppermute(left, Y, ring(yn, 1))
    own_col = jnp.concatenate([txt, left, right, far], axis=0)
    left_col = lax.ppermute(own_col, "x", ring(xn, 1))
    right_col = lax.ppermute(own_col, "x", ring(xn, xn - 1))
    far_a = lax.ppermute(left_col[:column // 2], "x", ring(xn, 1))
    far_b = lax.ppermute(right_col[column // 2:], "x", ring(xn, xn - 1))
    blocks = [(own_col,), (left_col,), (right_col,), (far_a, far_b)]
    blocks = [b + tuple(swap(v) for v in b) for b in blocks]

    timg, feats, simg, simgb, inv, self_col, diag = pl.pallas_call(
        functools.partial(images_kernel, zn, dt),
        in_specs=[SMEM] + [VMEM] * (2 + zn),
        out_specs=[VMEM] * 7,
        out_shape=[shape((images, dt), BF16), shape((images, feat), BF16), shape((images, ds), F32), shape((images, ds), BF16),
                   shape((images, LANES), F32), shape((images, LANES), F32), shape((rows, ds), F32)],
        compiler_params=params(),
        cost_estimate=cost(images * feat * ds, 9),
        name="images",
    )(place, st_own, proj, *pieces)

    span = column * cn
    part = images // 2
    by_rows = lambda n: pl.BlockSpec((part, n), lambda i: (i, 0))
    old = self_col
    chain = []
    cols = []
    for n, block in enumerate(blocks):
        first = n == 0
        at = lambda i, n=n: (i, n)
        big = [shape((images, texts), BF16)] * 3 + [shape((texts, ds), BF16)]
        out = pl.pallas_call(
            make_block(first, gain, [v.shape[0] for v in block]),
            grid=(2,),
            in_specs=[by_rows(dt), by_rows(ds), by_rows(LANES)]
            + [pl.BlockSpec(v.shape, lambda i: (0, 0)) for v in block]
            + ([] if first else [pl.BlockSpec(memory_space=pl.ANY)] * 4),
            out_specs=[pl.BlockSpec((part, span), at)] * 3 + [pl.BlockSpec((span, ds), lambda i, n=n: (n, 0)), by_rows(LANES), pl.BlockSpec((8, part), lambda i: (0, i))],
            out_shape=big + [shape((images, LANES), F32), shape((8, images), F32)],
            scratch_shapes=[pltpu.VMEM((part, span), F32)] * 2,
            input_output_aliases={} if first else {3 + len(block) + k: k for k in range(4)},
            compiler_params=params(),
            cost_estimate=cost(images * span * (dt + ds), 7, 4 * images * span),
            name="block" + str(n),
        )(timg, simgb, old, *block, *chain)
        chain, old, flat = list(out[:4]), out[4], out[5]
        cols.append(old)

    a, b, c, ft = pl.pallas_call(
        functools.partial(embed_kernel, len(cols)),
        grid=(2,),
        in_specs=[by_rows(texts)] * 3 + [pl.BlockSpec((texts, ds), lambda i: (0, 0)), by_rows(ds), by_rows(LANES), by_rows(feat)] + [by_rows(LANES)] * len(cols),
        out_specs=[by_rows(ds)] * 3 + [pl.BlockSpec((feat, part), lambda i: (0, i))],
        out_shape=[shape((images, ds), BF16)] * 3 + [shape((feat, images), BF16)],
        scratch_shapes=[pltpu.VMEM((part, texts), BF16)],
        compiler_params=params(),
        cost_estimate=cost(3 * images * texts * ds, 16),
        name="embed",
    )(*chain, simg, inv, feats, *cols)

    own = flat[:5]
    below = lax.ppermute(own, "z", ring(zn, 1))
    above = lax.ppermute(own, "z", ring(zn, zn - 1))
    pair = merge(own, above)
    window = merge(pair, below)
    ahead = lax.ppermute(window, "z", ring(zn, zn - 3))
    behind = lax.ppermute(pair, "z", ring(zn, 3))
    sums = merge(window, ahead, behind)

    away, hi, lo, val = pl.pallas_call(
        away_kernel,
        in_specs=[SMEM] + [VMEM] * 7,
        out_specs=[VMEM] * 4,
        out_shape=[shape((half + 8, ds), F32), shape((images, ds), BF16), shape((images, ds), BF16), shape((8, images), F32)],
        scratch_shapes=[pltpu.VMEM((images, LANES), F32), pltpu.VMEM((half, ds), F32), pltpu.VMEM((half, images), BF16)],
        compiler_params=params(),
        cost_estimate=cost(2 * images * half * ds, 8),
        name="away",
    )(place, sums, flat, a, b, c, diag, ft)
    arrived = swap(away)
    home = pl.pallas_call(
        home_kernel,
        in_specs=[SMEM] + [VMEM] * 3,
        out_specs=VMEM,
        out_shape=shape((half, ds), F32),
        scratch_shapes=[pltpu.VMEM((half, images), BF16)],
        compiler_params=params(),
        cost_estimate=cost(2 * images * half * ds, 4),
        name="home",
    )(place, ft, hi, lo)

    cut = half // xn
    keep, *sends = pl.pallas_call(
        functools.partial(cores_kernel, xn),
        in_specs=[SMEM] + [VMEM] * 3,
        out_specs=[VMEM] * 4,
        out_shape=[shape((cut + 8, ds), F32)] + [shape((cut + 16, ds), BF16)] * 3,
        compiler_params=params(),
        name="cores",
    )(place, home, arrived, away[half:])
    got = [lax.ppermute(v, "x", ring(xn, k)) for k, v in zip((1, 3, 2), sends)]
    mine, other = pl.pallas_call(
        rows_kernel,
        in_specs=[SMEM] + [VMEM] * 4,
        out_specs=[VMEM] * 2,
        out_shape=[shape((cut // 2 + 8, ds), F32)] * 2,
        scratch_shapes=[pltpu.VMEM((cut, ds), F32)],
        compiler_params=params(),
        name="rows",
    )(place, keep, *got)
    got = [lax.ppermute(other, Y, ring(yn, k)) for k in (1, 3)] + [lax.ppermute(mine, Y, ring(yn, 2))]
    plane = mine + got[0] + got[1] + got[2]

    below = lax.ppermute(plane, "z", ring(zn, 1))
    above = lax.ppermute(plane, "z", ring(zn, zn - 1))
    pair = plane + above
    window = pair + below
    ahead = lax.ppermute(window, "z", ring(zn, zn - 3))
    behind = lax.ppermute(pair, "z", ring(zn, 3))
    total = window + ahead + behind

    row_loss = lax.dynamic_slice_in_dim(val[0], lax.axis_index("z") * rows, rows, 0)
    return (row_loss, total[cut // 2, 0] / (batch * zn), total[:cut // 2])


def solution(mesh):
    sizes = dict(mesh.shape)
    fine = Mesh(np.asarray(mesh.devices).reshape(sizes["blk"] // 2, 2, sizes["img"] // 4, 2, 2), ALL)
    return jax.shard_map(
        per_device,
        mesh=fine,
        in_specs=(P(ALL, None), P(), P(ALL, None), P(ALL, None), P(ALL, None)),
        out_specs=(P(ALL), P(), P(("x", "yl", "c"), None)),
        check_vma=False,
    )
```

```python
import functools

import jax
import jax.numpy as jnp
import numpy as np
from jax import lax
from jax.experimental import pallas as pl
from jax.experimental.pallas import tpu as pltpu
from jax.sharding import Mesh, PartitionSpec as P

sig_scale = 10.0
sig_bias = -10.0
teacher_gain = 3.0
eps_value = 1e-06

F32 = jnp.float32
BF16 = jnp.bfloat16
LOG2E = float(np.log2(np.e))
LN2 = float(np.log(2.0))
NT = (((1,), (1,)), ((), ()))
ALL = ("z", "yh", "x", "yl", "c")
Y = ("yh", "yl")
VMEM_LIMIT = 8 * 1024 * 1024
OWN_LIMIT = 63 * 1024 * 1024
LANES = 128
STEP = 8
PART = 128


def ring(n, k):
    return [(i, (i + k) % n) for i in range(n)]


def flip(n, k):
    return [(i, i ^ k) for i in range(n)]


SMEM = pl.BlockSpec(memory_space=pltpu.SMEM)
VMEM = pl.BlockSpec(memory_space=pltpu.VMEM)


def shape(dims, dtype):
    return jax.ShapeDtypeStruct(dims, dtype)


def params():
    return pltpu.CompilerParams(vmem_limit_bytes=VMEM_LIMIT)


def cost(macs, megabytes, exps=0):
    return pl.CostEstimate(flops=int(2 * macs), bytes_accessed=int(megabytes * 1e6), transcendentals=int(exps))


def own_kernel(place_ref, feat_ref, txt_ref, timg_ref, ttxt_ref, msg_ref, half_ref, img_ref, stxt_ref, pair, raw, sems):
    dt = ttxt_ref.shape[1]
    half = half_ref.shape[0]
    copies = [
        pltpu.make_async_copy(txt_ref, raw, sems.at[0]),
        pltpu.make_async_copy(ttxt_ref, pair.at[:, :dt], sems.at[1]),
        pltpu.make_async_copy(timg_ref, img_ref.at[:, :dt], sems.at[2]),
        pltpu.make_async_copy(feat_ref, img_ref.at[:, dt:], sems.at[3]),
    ]
    for copy in copies:
        copy.start()
    copies[0].wait()
    txt = raw[...].astype(F32)
    txt = txt / jnp.sqrt(jnp.sum(txt * txt, axis=1, keepdims=True) + eps_value)
    stxt_ref[...] = txt.astype(BF16)
    pair[:, dt:] = stxt_ref[...]
    for copy in copies[1:]:
        copy.wait()
    core = place_ref[1]
    half_ref[...] = pair[pl.ds(pl.multiple_of(core * half, half), half), :]
    msg_ref[:half, :] = pair[pl.ds(pl.multiple_of((1 - core) * half, half), half), :]
    msg_ref[half:, :] = img_ref[...]


def chip_kernel(half_ref, img_ref, got_ref, txts_ref, imgs_ref):
    half, rows = half_ref.shape[0], img_ref.shape[0]
    txts_ref[:half, :] = half_ref[...]
    txts_ref[half:, :] = got_ref[:half, :]
    imgs_ref[:rows, :] = img_ref[...]
    imgs_ref[rows:, :] = got_ref[half:, :]


def column_kernel(a_ref, b_ref, c_ref, d_ref, out_ref):
    rows = a_ref.shape[0]
    for n, ref in enumerate((a_ref, b_ref, c_ref, d_ref)):
        out_ref[n * rows:(n + 1) * rows, :] = ref[...]


def images_kernel(zn, dt, place_ref, own_txt_ref, proj_ref, *refs):
    count = zn // 2 - 1
    img_ref, mine, theirs, last_ref = refs[0], refs[1:1 + count], refs[1 + count:1 + 2 * count], refs[1 + 2 * count]
    timg_ref, feat_ref, simg_ref, simgb_ref, inv_ref, self_ref, diag_ref = refs[2 + 2 * count:]
    rows = img_ref.shape[0]
    z = place_ref[0]
    side = 1 - 2 * place_ref[1]

    def put(ref, shift):
        at = pl.ds(pl.multiple_of(lax.rem(z + shift + zn, zn) * rows, rows), rows)
        timg_ref[at, :] = ref[:rows, :dt]
        feat_ref[at, :] = ref[:rows, dt:]

    put(img_ref, 0)
    for k in range(count):
        put(mine[k], -side * (k + 1))
        put(theirs[k], side * (k + 1))
    put(last_ref, zn // 2)
    pre = jnp.dot(feat_ref[...], proj_ref[...], preferred_element_type=F32)
    norm = jnp.sqrt(jnp.sum(pre * pre, axis=1, keepdims=True) + eps_value)
    simg = pre / norm
    simg_ref[...] = simg
    simgb_ref[...] = simg.astype(BF16)
    inv_ref[...] = jnp.broadcast_to(1.0 / norm, inv_ref.shape)
    own = pl.ds(pl.multiple_of(z * rows, rows), rows)
    s = simg_ref[own, :]
    txt = own_txt_ref[...].astype(F32)
    margin = sig_scale * jnp.sum(s.astype(BF16).astype(F32) * txt, axis=1, keepdims=True) + sig_bias
    self_ref[...] = jnp.zeros_like(self_ref)
    lane = lax.broadcasted_iota(jnp.int32, (rows, LANES), 1)
    self_ref[own, :] = jnp.where(lane == 0, -margin, 0.0)
    d = -sig_scale * txt
    diag_ref[...] = (d - s * jnp.sum(s * d, axis=1, keepdims=True)) * inv_ref[own, 0:1]


def make_block(index, last, gain, sizes):
    first = index == 0
    span = sum(sizes)

    def kernel(timg_ref, simgb_ref, old_ref, *refs):
        texts, refs = refs[:len(sizes)], refs[len(sizes):]
        if not first:
            refs = refs[4:]
        te_ref, se_ref, sig_ref, stu_ref, stat_ref, top_ref = refs[:6]
        flat_ref = refs[6] if last else None
        tl, sl = refs[-2:]
        dt = timg_ref.shape[1]
        images = timg_ref.shape[0]
        cols = slice(index * span, (index + 1) * span)
        shrink = float(np.exp(sig_bias))
        fold = lambda v: sum((v[:, k:k + LANES] for k in range(LANES, span, LANES)), v[:, :LANES])
        at = 0
        for ref, n in zip(texts, sizes):
            stu_ref[index * span + at:index * span + at + n, :] = ref[:, dt:]
            at += n
        for p in range(0, images, PART):
            part = slice(p, p + PART)
            at = 0
            for ref, n in zip(texts, sizes):
                tl[part, at:at + n] = lax.dot_general(timg_ref[part, :], ref[:, :dt], NT, preferred_element_type=F32)
                sl[part, at:at + n] = lax.dot_general(simgb_ref[part, :], ref[:, dt:], NT, preferred_element_type=F32)
                at += n
            for r in range(p, p + PART, STEP):
                rows = slice(r, r + STEP)
                t = (gain * LOG2E) * tl[rows, :]
                s = (sig_scale * LOG2E) * sl[rows, :]
                top = jnp.max(t, axis=1, keepdims=True)
                if not first:
                    top = jnp.maximum(top, old_ref[rows, :LANES])
                top = jnp.broadcast_to(top, (STEP, LANES))
                te = jnp.exp2(t - jnp.concatenate([top] * (span // LANES), axis=1))
                se = jnp.exp2(s)
                em = se * shrink
                up = 1.0 + em
                sig = em * pl.reciprocal(up, approx=True)
                soft = jnp.log(up) + (em - (up - 1.0))
                te_ref[rows, cols] = te.astype(BF16)
                se_ref[rows, cols] = se.astype(BF16)
                sig_ref[rows, cols] = sig.astype(BF16)
                sums = [fold(te), fold(se), fold(te * (t - s)), fold(soft)]
                if first:
                    sums[3] = sums[3] + old_ref[rows, :]
                else:
                    w = jnp.exp2(old_ref[rows, :LANES] - top)
                    was = [old_ref[rows, k * LANES:(k + 1) * LANES] for k in range(1, 5)]
                    sums = [sums[0] + w * was[0], sums[1] + was[1], sums[2] + w * was[2], sums[3] + was[3]]
                top_ref[rows, :] = top
                for k, v in enumerate([top] + sums):
                    stat_ref[rows, k * LANES:(k + 1) * LANES] = v
        if last:
            ones = jnp.ones((8, LANES), F32)
            out = [stat_ref[:, :LANES].T[:1, :]]
            for k in range(1, 5):
                v = lax.dot_general(ones, stat_ref[:, k * LANES:(k + 1) * LANES], NT, precision=lax.Precision.HIGHEST, preferred_element_type=F32)
                out.append(v[:1, :])
            flat_ref[...] = jnp.concatenate(out + [jnp.zeros((3, images), F32)], axis=0)

    return kernel


def carry(weights, txt, simg, inv):
    d = jnp.dot(weights, txt, preferred_element_type=F32)
    along = jnp.sum(simg * d, axis=1, keepdims=True)
    return ((d - simg * along) * inv).astype(BF16)


def student_kernel(se_ref, sig_ref, stu_ref, simg_ref, inv_ref, feat_ref, a_ref, c_ref, ft_ref, done_ref):
    simg = simg_ref[...]
    inv = inv_ref[:, 0:1]
    a_ref[...] = carry(se_ref[...], stu_ref[...], simg, inv)
    c_ref[...] = carry(sig_ref[...], stu_ref[...], simg, inv)
    ft_ref[...] = feat_ref[...].T
    done_ref[...] = jnp.zeros_like(done_ref)


def teacher_kernel(te_ref, stu_ref, simg_ref, inv_ref, *refs):
    stats, (b_ref, scaled) = refs[:-2], refs[-2:]
    span = te_ref.shape[1] // len(stats)
    top = stats[-1][:, 0:1]
    for n, stat in enumerate(stats):
        cols = slice(n * span, (n + 1) * span)
        w = jnp.exp2(stat[:, 0:1] - top)
        scaled[:, cols] = (te_ref[:, cols].astype(F32) * w).astype(BF16)
    b_ref[...] = carry(scaled[...], stu_ref[...], simg_ref[...], inv_ref[:, 0:1])


def away_kernel(place_ref, window_ref, ahead_ref, behind_ref, flat_ref, a_ref, b_ref, c_ref, diag_ref, ft_ref,
                out_ref, hi_ref, lo_ref, val_ref, turned, cut_ft):
    rows = diag_ref.shape[0]
    half, ds = cut_ft.shape[0], a_ref.shape[1]
    sums = merge(window_ref[...], ahead_ref[...], behind_ref[...])
    top, tsum, ssum, tval, soft = (sums[k:k + 1, :] for k in range(5))
    value = tval / tsum * LN2 + soft - (top * LN2 + jnp.log(tsum)) + jnp.log(ssum)
    val_ref[...] = jnp.broadcast_to(value, val_ref.shape)
    ca = sig_scale / ssum
    cb = -sig_scale * jnp.exp2(flat_ref[0:1, :] - top) / tsum
    row = lax.broadcasted_iota(jnp.int32, (LANES, ca.shape[1]), 0)
    turned[...] = jnp.where(row == 0, ca, cb).T
    d = turned[:, 0:1] * a_ref[...].astype(F32) + turned[:, 1:2] * b_ref[...].astype(F32) + sig_scale * c_ref[...].astype(F32)
    hi_ref[...] = d.astype(BF16)
    lo_ref[...] = (d - hi_ref[...].astype(F32)).astype(BF16)
    own = pl.ds(pl.multiple_of(place_ref[0] * rows, rows), rows)
    mine = hi_ref[own, :].astype(F32) + lo_ref[own, :].astype(F32) + diag_ref[...]
    mine_hi = mine.astype(BF16)
    hi_ref[own, :] = mine_hi
    lo_ref[own, :] = (mine - mine_hi.astype(F32)).astype(BF16)
    pick(cut_ft, ft_ref, 1 - place_ref[1])
    g = jnp.dot(cut_ft[...], hi_ref[...], preferred_element_type=F32)
    out_ref[:half, :] = g + jnp.dot(cut_ft[...], lo_ref[...], preferred_element_type=F32)
    out_ref[half:, :] = jnp.broadcast_to(jnp.sum(value, axis=1, keepdims=True), (8, ds))


def pick(dst, src, core):
    groups = 8
    cut = dst.shape[0] // groups
    for g in range(groups):
        dst[g * cut:(g + 1) * cut, :] = src[pl.ds(pl.multiple_of((2 * g + core) * cut, cut), cut), :]


def home_kernel(place_ref, ft_ref, hi_ref, lo_ref, out_ref, cut_ft):
    pick(cut_ft, ft_ref, place_ref[1])
    out_ref[...] = jnp.dot(cut_ft[...], hi_ref[...], preferred_element_type=F32) + jnp.dot(
        cut_ft[...], lo_ref[...], preferred_element_type=F32)


def packed(loss):
    hi = loss.astype(BF16).astype(F32)
    mid = (loss - hi).astype(BF16).astype(F32)
    low = loss - hi - mid
    row = lax.broadcasted_iota(jnp.int32, loss.shape, 0)
    out = jnp.where(row == 0, hi, jnp.where(row == 1, mid, jnp.where(row == 2, low, 0.0)))
    return jnp.concatenate([out, jnp.zeros_like(out)], axis=0).astype(BF16)


def unpacked(rows):
    rows = rows.astype(F32)
    return rows[0:1, :] + rows[1:2, :] + rows[2:3, :]


def cores_kernel(xn, place_ref, home_ref, got_ref, away_ref, keep_ref, *sends):
    half = home_ref.shape[0]
    cut = half // xn
    loss = got_ref[half:, :] + away_ref[half:, :]
    x = place_ref[2]
    at = pl.ds(pl.multiple_of(x * cut, cut), cut)
    keep_ref[:cut, :] = home_ref[at, :] + got_ref[at, :]
    keep_ref[cut:, :] = loss
    rows = packed(loss)
    for k, ref in zip((1, 3, 2), sends):
        at = pl.ds(pl.multiple_of(lax.rem(x + k, xn) * cut, cut), cut)
        ref[:cut, :] = (home_ref[at, :] + got_ref[at, :]).astype(BF16)
        ref[cut:, :] = rows


def rows_kernel(place_ref, keep_ref, p_ref, q_ref, r_ref, mine_ref, across_ref, other_ref, total):
    cut = keep_ref.shape[0] - 8
    half = cut // 2
    total[...] = keep_ref[:cut, :]
    loss = keep_ref[cut:, :]
    for ref in (p_ref, q_ref, r_ref):
        total[...] += ref[:cut, :].astype(F32)
        loss = loss + unpacked(ref[cut:, :])
    y = place_ref[3]
    mine_ref[:half, :] = total[pl.ds(pl.multiple_of(y * half, half), half), :]
    mine_ref[half:, :] = loss
    across_ref[:half, :] = mine_ref[:half, :].astype(BF16)
    across_ref[half:, :] = packed(loss)
    other_ref[:half, :] = total[pl.ds(pl.multiple_of((1 - y) * half, half), half), :]
    other_ref[half:, :] = loss


def plane_kernel(mine_ref, p_ref, q_ref, r_ref, out_ref, loss_ref):
    half = out_ref.shape[0]
    out_ref[...] = mine_ref[:half, :] + p_ref[:half, :] + q_ref[:half, :] + r_ref[:half, :].astype(F32)
    loss = mine_ref[half:, :] + p_ref[half:, :] + q_ref[half:, :] + unpacked(r_ref[half:, :])
    loss_ref[...] = loss[:, :LANES]


def merge(*parts):
    top = functools.reduce(jnp.maximum, [p[0:1, :] for p in parts])
    out = [0.0] * 4
    for p in parts:
        w = jnp.exp2(p[0:1, :] - top)
        out = [out[0] + w * p[1:2, :], out[1] + p[2:3, :], out[2] + w * p[3:4, :], out[3] + p[4:5, :]]
    return jnp.concatenate([top] + out + [jnp.zeros((3, top.shape[1]), F32)], axis=0)


def near_kernel(own_ref, above_ref, below_ref, after_ref, pair_ref, window_ref):
    pair = merge(own_ref[...], above_ref[...])
    pair_ref[...] = pair
    window_ref[...] = merge(pair, below_ref[...])


def per_device(features, proj, student_text, teacher_image, teacher_text):
    rows, feat = features.shape
    dt = teacher_text.shape[1]
    ds = student_text.shape[1]
    zn, yn, xn, cn = (lax.axis_size(a) for a in ("z", Y, "x", "c"))
    images = rows * zn
    batch = images * yn * xn * cn
    texts = rows * yn * xn * cn
    column = rows * yn
    gain = float(teacher_gain / np.sqrt(np.float32(dt)))
    half = feat // cn
    place = jnp.stack([lax.axis_index(a) for a in ("z", "c", "x", "yl")]).astype(jnp.int32)

    swap = lambda v: lax.ppermute(v, "c", flip(cn, 1))
    msg, half_txt, img, st_own = pl.pallas_call(
        own_kernel,
        in_specs=[SMEM] + [pl.BlockSpec(memory_space=pltpu.HBM)] * 4,
        out_specs=[VMEM] * 4,
        out_shape=[shape((rows + rows // 2, dt + feat), BF16), shape((rows // 2, dt + ds), BF16), shape((rows, dt + feat), BF16), shape((rows, ds), BF16)],
        scratch_shapes=[pltpu.VMEM((rows, dt + ds), BF16), pltpu.VMEM((rows, ds), BF16), pltpu.SemaphoreType.DMA((4,))],
        compiler_params=pltpu.CompilerParams(vmem_limit_bytes=OWN_LIMIT),
        name="own",
    )(place, features, student_text, teacher_image, teacher_text)
    txts, imgs = pl.pallas_call(
        chip_kernel,
        in_specs=[VMEM] * 3,
        out_specs=[VMEM] * 2,
        out_shape=[shape((rows, dt + ds), BF16), shape((2 * rows, dt + feat), BF16)],
        compiler_params=params(),
        name="chip",
    )(half_txt, img, swap(msg))

    def plane(v, step, stage):
        pairs = []
        dims = (yn // 2, xn, 2, cn)
        for src in np.ndindex(*dims):
            yh, x, yl, c = src
            y = 2 * yh + yl
            if c == stage:
                y = (y + step) % yn
            else:
                x = (x + step) % xn
            dst = (y // 2, x, y % 2, c)
            pairs.append((int(np.ravel_multi_index(src, dims)), int(np.ravel_multi_index(dst, dims))))
        return lax.ppermute(v, ("yh", "x", "yl", "c"), pairs)

    def climb(v):
        pairs = [(z * cn + c, (z + (1 if c == 0 else -1)) % zn * cn + c) for z in range(zn) for c in range(cn)]
        return lax.ppermute(v, ("z", "c"), pairs)

    together = lax.optimization_barrier
    step1, left, right = together((climb(imgs), plane(txts, 1, 0), plane(txts, -1, 0)))
    step2, far = climb(step1), plane(left, 1, 0)
    own_col = pl.pallas_call(
        column_kernel,
        in_specs=[VMEM] * 4,
        out_specs=VMEM,
        out_shape=shape((column, dt + ds), BF16),
        compiler_params=params(),
        name="column",
    )(txts, left, right, far)
    step3 = climb(step2)
    mine = [step1, step2, step3]
    theirs = [swap(v[rows:]) for v in mine[:2]] + [None]
    left_col, right_col, step3, swap1, swap2 = together((plane(own_col, 1, 1), plane(own_col, -1, 1), step3, *theirs[:2]))
    theirs = [swap1, swap2, swap(step3[rows:])]
    mine[2] = step3
    last_img = climb(step3[:rows])
    far_a = plane(left_col[:column // 2], 1, 1)
    far_b = plane(right_col[column // 2:], -1, 1)

    timg, feats, simg, simgb, inv, self_col, diag = pl.pallas_call(
        functools.partial(images_kernel, zn, dt),
        in_specs=[SMEM] + [VMEM] * (4 + 2 * len(mine)),
        out_specs=[VMEM] * 7,
        out_shape=[shape((images, dt), BF16), shape((images, feat), BF16), shape((images, ds), F32), shape((images, ds), BF16),
                   shape((images, LANES), F32), shape((images, LANES), F32), shape((rows, ds), F32)],
        compiler_params=params(),
        cost_estimate=cost(images * feat * ds, 9),
        name="images",
    )(place, st_own, proj, img, *mine, *theirs, last_img)

    blocks = [(own_col, swap(own_col)), (left_col, swap(left_col)), (right_col, swap(right_col)), None]
    span = column * cn
    stat = self_col
    chain = []
    stats = []
    for n, block in enumerate(blocks):
        final = n == len(blocks) - 1
        if final:
            block = (far_a, far_b, swap(far_a), swap(far_b))
        big = [shape((images, texts), BF16)] * 3 + [shape((texts, ds), BF16), shape((images, 5 * LANES), F32), shape((images, LANES), F32)]
        out = pl.pallas_call(
            make_block(n, final, gain, [v.shape[0] for v in block]),
            in_specs=[VMEM] * (3 + len(block) + len(chain)),
            out_specs=[VMEM] * (7 if final else 6),
            out_shape=big + ([shape((8, images), F32)] if final else []),
            scratch_shapes=[pltpu.VMEM((images, span), F32)] * 2,
            input_output_aliases={3 + len(block) + k: k for k in range(len(chain))} | ({2: 4} if n else {}),
            compiler_params=params(),
            cost_estimate=cost(images * span * (dt + ds), 7, 4 * images * span),
            name="block" + str(n),
        )(timg, simgb, stat, *block, *chain)
        chain, stat = list(out[:4]), out[4]
        stats.append(out[5])
        if n == 1:
            far_a, far_b, stat = together((far_a, far_b, stat))
    flat = out[6]
    te, se, sig, stu = chain

    a, c, ft, done_student = pl.pallas_call(
        student_kernel,
        in_specs=[VMEM] * 6,
        out_specs=[VMEM] * 4,
        out_shape=[shape((images, ds), BF16)] * 2 + [shape((feat, images), BF16), shape((8, LANES), F32)],
        compiler_params=params(),
        cost_estimate=cost(2 * images * texts * ds, 8),
        name="student",
    )(se, sig, stu, simg, inv, feats)
    b = pl.pallas_call(
        teacher_kernel,
        in_specs=[VMEM] * (4 + len(stats)),
        out_specs=VMEM,
        out_shape=shape((images, ds), BF16),
        scratch_shapes=[pltpu.VMEM((images, texts), BF16)],
        compiler_params=params(),
        cost_estimate=cost(images * texts * ds, 8),
        name="teacher",
    )(te, stu, simg, inv, *stats)

    below = lax.ppermute(flat, "z", ring(zn, 1))
    above = lax.ppermute(flat, "z", ring(zn, zn - 1))
    pair, window = pl.pallas_call(
        near_kernel,
        in_specs=[VMEM] * 4,
        out_specs=[VMEM] * 2,
        out_shape=[shape((8, images), F32)] * 2,
        compiler_params=params(),
        name="near",
    )(flat, above, below, done_student)
    ahead = lax.ppermute(window, "z", ring(zn, zn - 3))
    behind = lax.ppermute(pair, "z", ring(zn, 3))

    away, hi, lo, val = pl.pallas_call(
        away_kernel,
        in_specs=[SMEM] + [VMEM] * 9,
        out_specs=[VMEM] * 4,
        out_shape=[shape((half + 8, ds), F32), shape((images, ds), BF16), shape((images, ds), BF16), shape((8, images), F32)],
        scratch_shapes=[pltpu.VMEM((images, LANES), F32), pltpu.VMEM((half, images), BF16)],
        compiler_params=params(),
        cost_estimate=cost(2 * images * half * ds, 8),
        name="away",
    )(place, window, ahead, behind, flat, a, b, c, diag, ft)
    arrived = swap(away)
    home = pl.pallas_call(
        home_kernel,
        in_specs=[SMEM] + [VMEM] * 3,
        out_specs=VMEM,
        out_shape=shape((half, ds), F32),
        scratch_shapes=[pltpu.VMEM((half, images), BF16)],
        compiler_params=params(),
        cost_estimate=cost(2 * images * half * ds, 4),
        name="home",
    )(place, ft, hi, lo)

    cut = half // xn
    keep, *sends = pl.pallas_call(
        functools.partial(cores_kernel, xn),
        in_specs=[SMEM] + [VMEM] * 3,
        out_specs=[VMEM] * 4,
        out_shape=[shape((cut + 8, ds), F32)] + [shape((cut + 16, ds), BF16)] * 3,
        compiler_params=params(),
        name="cores",
    )(place, home, arrived, away)
    got = [lax.ppermute(v, "x", ring(xn, k)) for k, v in zip((1, 3, 2), sends)]
    cut = cut // 2
    mine, across, other = pl.pallas_call(
        rows_kernel,
        in_specs=[SMEM] + [VMEM] * 4,
        out_specs=[VMEM] * 3,
        out_shape=[shape((cut + 8, ds), F32), shape((cut + 16, ds), BF16), shape((cut + 8, ds), F32)],
        scratch_shapes=[pltpu.VMEM((2 * cut, ds), F32)],
        compiler_params=params(),
        name="rows",
    )(place, keep, *got)
    own, loss = pl.pallas_call(
        plane_kernel,
        in_specs=[VMEM] * 4,
        out_specs=[VMEM] * 2,
        out_shape=[shape((cut, ds), F32), shape((8, LANES), F32)],
        compiler_params=params(),
        name="plane",
    )(mine, lax.ppermute(other, Y, ring(yn, 1)), lax.ppermute(other, Y, ring(yn, 3)), lax.ppermute(across, Y, ring(yn, 2)))

    below = lax.ppermute(own, "z", ring(zn, 1))
    above = lax.ppermute(own, "z", ring(zn, zn - 1))
    pair = own + above
    window = pair + below
    ahead = lax.ppermute(window.astype(BF16), "z", ring(zn, zn - 3))
    behind = lax.ppermute(pair.astype(BF16), "z", ring(zn, 3))
    grad = window + ahead.astype(F32) + behind.astype(F32)

    row_loss = lax.dynamic_slice_in_dim(val[0], lax.axis_index("z") * rows, rows, 0)
    return (row_loss, loss[0, 0] / batch, grad)


def solution(mesh):
    sizes = dict(mesh.shape)
    fine = Mesh(np.asarray(mesh.devices).reshape(sizes["blk"] // 2, 2, sizes["img"] // 4, 2, 2), ALL)
    return jax.shard_map(
        per_device,
        mesh=fine,
        in_specs=(P(ALL, None), P(), P(ALL, None), P(ALL, None), P(ALL, None)),
        out_specs=(P(ALL), P(), P(("x", "yl", "c"), None)),
        check_vma=False,
    )
```

```python
import functools

import jax
import jax.numpy as jnp
import numpy as np
from jax import lax
from jax.experimental import pallas as pl
from jax.experimental.pallas import tpu as pltpu
from jax.sharding import Mesh, PartitionSpec as P

sig_scale = 10.0
sig_bias = -10.0
teacher_gain = 3.0
eps_value = 1e-06

F32 = jnp.float32
BF16 = jnp.bfloat16
LOG2E = float(np.log2(np.e))
LN2 = float(np.log(2.0))
NT = (((1,), (1,)), ((), ()))
ALL = ("z", "yh", "x", "yl", "c")
Y = ("yh", "yl")
VMEM_LIMIT = 8 * 1024 * 1024
FREE = pl.CostEstimate(flops=1, bytes_accessed=1, transcendentals=0)
LANES = 128
STEP = 8
PART = 128


def ring(n, k):
    return [(i, (i + k) % n) for i in range(n)]


def flip(n, k):
    return [(i, i ^ k) for i in range(n)]


SMEM = pl.BlockSpec(memory_space=pltpu.SMEM)
VMEM = pl.BlockSpec(memory_space=pltpu.VMEM)


def shape(dims, dtype):
    return jax.ShapeDtypeStruct(dims, dtype)


def params():
    return pltpu.CompilerParams(vmem_limit_bytes=VMEM_LIMIT)


def chip_kernel(place_ref, img_ref, txt_ref, feat2_ref, txt2_ref, timg2_ref, ttxt2_ref, txts_ref, imgs_ref, stxt_ref):
    rows, dt = ttxt2_ref.shape
    half = rows // 2
    mine = pl.ds(pl.multiple_of(place_ref[1] * half, half), half)
    stxt_ref[...] = unit(txt_ref[:, dt:])
    txts_ref[:half, :dt] = txt_ref[mine, :dt]
    txts_ref[half:, :dt] = ttxt2_ref[mine, :]
    txts_ref[:half, dt:] = stxt_ref[mine, :]
    txts_ref[half:, dt:] = unit(txt2_ref[mine, :])
    imgs_ref[:rows, :] = img_ref[...]
    imgs_ref[rows:, :dt] = timg2_ref[...]
    imgs_ref[rows:, dt:] = feat2_ref[...]


def unit(txt):
    txt = txt.astype(F32)
    return (txt / jnp.sqrt(jnp.sum(txt * txt, axis=1, keepdims=True) + eps_value)).astype(BF16)


def column_kernel(a_ref, b_ref, c_ref, d_ref, out_ref):
    rows = a_ref.shape[0]
    for n, ref in enumerate((a_ref, b_ref, c_ref, d_ref)):
        out_ref[n * rows:(n + 1) * rows, :] = ref[...]


def images_kernel(zn, dt, place_ref, own_txt_ref, proj_ref, *refs):
    count = zn // 2 - 1
    img_ref, mine, theirs, last_ref = refs[0], refs[1:1 + count], refs[1 + count:1 + 2 * count], refs[1 + 2 * count]
    timg_ref, feat_ref, simg_ref, simgb_ref, inv_ref, self_ref, diag_ref = refs[2 + 2 * count:]
    rows = img_ref.shape[0] // 2
    z = place_ref[0]
    side = 1 - 2 * place_ref[1]

    def put(ref, shift):
        at = pl.ds(pl.multiple_of(lax.rem(z + shift + zn, zn) * rows, rows), rows)
        timg_ref[at, :] = ref[:rows, :dt]
        feat_ref[at, :] = ref[:rows, dt:]

    put(img_ref, 0)
    for k in range(count):
        put(mine[k], -side * (k + 1))
        put(theirs[k], side * (k + 1))
    put(last_ref, zn // 2)
    pre = jnp.dot(feat_ref[...], proj_ref[...], preferred_element_type=F32)
    norm = jnp.sqrt(jnp.sum(pre * pre, axis=1, keepdims=True) + eps_value)
    simg = pre / norm
    simg_ref[...] = simg
    simgb_ref[...] = simg.astype(BF16)
    inv_ref[...] = jnp.broadcast_to(1.0 / norm, inv_ref.shape)
    own = pl.ds(pl.multiple_of(z * rows, rows), rows)
    s = simg_ref[own, :]
    txt = own_txt_ref[...].astype(F32)
    margin = sig_scale * jnp.sum(s.astype(BF16).astype(F32) * txt, axis=1, keepdims=True) + sig_bias
    self_ref[...] = jnp.zeros_like(self_ref)
    lane = lax.broadcasted_iota(jnp.int32, (rows, LANES), 1)
    self_ref[own, :] = jnp.where(lane == 0, -margin, 0.0)
    d = -sig_scale * txt
    diag_ref[...] = (d - s * jnp.sum(s * d, axis=1, keepdims=True)) * inv_ref[own, 0:1]


def make_block(index, last, gain, sizes):
    first = index == 0
    span = sum(sizes)

    def kernel(timg_ref, simgb_ref, old_ref, *refs):
        texts, refs = refs[:len(sizes)], refs[len(sizes):]
        if not first:
            refs = refs[4:]
        te_ref, se_ref, sig_ref, stu_ref, stat_ref, top_ref = refs[:6]
        flat_ref = refs[6] if last else None
        tl, sl = refs[-2:]
        dt = timg_ref.shape[1]
        images = timg_ref.shape[0]
        cols = slice(index * span, (index + 1) * span)
        shrink = float(np.exp(sig_bias))
        fold = lambda v: sum((v[:, k:k + LANES] for k in range(LANES, span, LANES)), v[:, :LANES])
        at = 0
        for ref, n in zip(texts, sizes):
            stu_ref[index * span + at:index * span + at + n, :] = ref[:, dt:]
            at += n
        for p in range(0, images, PART):
            part = slice(p, p + PART)
            at = 0
            for ref, n in zip(texts, sizes):
                tl[part, at:at + n] = lax.dot_general(timg_ref[part, :], ref[:, :dt], NT, preferred_element_type=F32)
                sl[part, at:at + n] = lax.dot_general(simgb_ref[part, :], ref[:, dt:], NT, preferred_element_type=F32)
                at += n
            for r in range(p, p + PART, STEP):
                rows = slice(r, r + STEP)
                t = (gain * LOG2E) * tl[rows, :]
                s = (sig_scale * LOG2E) * sl[rows, :]
                top = jnp.max(t, axis=1, keepdims=True)
                if not first:
                    top = jnp.maximum(top, old_ref[rows, :LANES])
                top = jnp.broadcast_to(top, (STEP, LANES))
                te = jnp.exp2(t - jnp.concatenate([top] * (span // LANES), axis=1))
                se = jnp.exp2(s)
                em = se * shrink
                up = 1.0 + em
                sig = em * pl.reciprocal(up, approx=True)
                soft = jnp.log(up) + (em - (up - 1.0))
                te_ref[rows, cols] = te.astype(BF16)
                se_ref[rows, cols] = se.astype(BF16)
                sig_ref[rows, cols] = sig.astype(BF16)
                sums = [fold(te), fold(se), fold(te * (t - s)), fold(soft)]
                if first:
                    sums[3] = sums[3] + old_ref[rows, :]
                else:
                    w = jnp.exp2(old_ref[rows, :LANES] - top)
                    was = [old_ref[rows, k * LANES:(k + 1) * LANES] for k in range(1, 5)]
                    sums = [sums[0] + w * was[0], sums[1] + was[1], sums[2] + w * was[2], sums[3] + was[3]]
                top_ref[rows, :] = top
                for k, v in enumerate([top] + sums):
                    stat_ref[rows, k * LANES:(k + 1) * LANES] = v
        if last:
            ones = jnp.ones((8, LANES), F32)
            out = [stat_ref[:, :LANES].T[:1, :]]
            for k in range(1, 5):
                v = lax.dot_general(ones, stat_ref[:, k * LANES:(k + 1) * LANES], NT, precision=lax.Precision.HIGHEST, preferred_element_type=F32)
                out.append(v[:1, :])
            flat_ref[...] = jnp.concatenate(out + [jnp.zeros((3, images), F32)], axis=0)

    return kernel


def carry(weights, txt, simg, inv):
    d = jnp.dot(weights, txt, preferred_element_type=F32)
    along = jnp.sum(simg * d, axis=1, keepdims=True)
    return ((d - simg * along) * inv).astype(BF16)


def student_kernel(se_ref, sig_ref, stu_ref, simg_ref, inv_ref, feat_ref, a_ref, c_ref, ft_ref, done_ref):
    simg = simg_ref[...]
    inv = inv_ref[:, 0:1]
    a_ref[...] = carry(se_ref[...], stu_ref[...], simg, inv)
    c_ref[...] = carry(sig_ref[...], stu_ref[...], simg, inv)
    ft_ref[...] = feat_ref[...].T
    done_ref[...] = jnp.zeros_like(done_ref)


def teacher_kernel(te_ref, stu_ref, simg_ref, inv_ref, *refs):
    stats, (b_ref, scaled) = refs[:-2], refs[-2:]
    span = te_ref.shape[1] // len(stats)
    top = stats[-1][:, 0:1]
    for n, stat in enumerate(stats):
        cols = slice(n * span, (n + 1) * span)
        w = jnp.exp2(stat[:, 0:1] - top)
        scaled[:, cols] = (te_ref[:, cols].astype(F32) * w).astype(BF16)
    b_ref[...] = carry(scaled[...], stu_ref[...], simg_ref[...], inv_ref[:, 0:1])


def away_kernel(place_ref, window_ref, ahead_ref, behind_ref, flat_ref, a_ref, b_ref, c_ref, diag_ref, ft_ref,
                out_ref, hi_ref, lo_ref, val_ref, turned, cut_ft):
    rows = diag_ref.shape[0]
    half, ds = cut_ft.shape[0], a_ref.shape[1]
    sums = merge(window_ref[...], ahead_ref[...], behind_ref[...])
    top, tsum, ssum, tval, soft = (sums[k:k + 1, :] for k in range(5))
    value = tval / tsum * LN2 + soft - (top * LN2 + jnp.log(tsum)) + jnp.log(ssum)
    val_ref[...] = jnp.broadcast_to(value, val_ref.shape)
    ca = sig_scale / ssum
    cb = -sig_scale * jnp.exp2(flat_ref[0:1, :] - top) / tsum
    row = lax.broadcasted_iota(jnp.int32, (LANES, ca.shape[1]), 0)
    turned[...] = jnp.where(row == 0, ca, cb).T
    d = turned[:, 0:1] * a_ref[...].astype(F32) + turned[:, 1:2] * b_ref[...].astype(F32) + sig_scale * c_ref[...].astype(F32)
    hi_ref[...] = d.astype(BF16)
    lo_ref[...] = (d - hi_ref[...].astype(F32)).astype(BF16)
    own = pl.ds(pl.multiple_of(place_ref[0] * rows, rows), rows)
    mine = hi_ref[own, :].astype(F32) + lo_ref[own, :].astype(F32) + diag_ref[...]
    mine_hi = mine.astype(BF16)
    hi_ref[own, :] = mine_hi
    lo_ref[own, :] = (mine - mine_hi.astype(F32)).astype(BF16)
    pick(cut_ft, ft_ref, 1 - place_ref[1])
    g = jnp.dot(cut_ft[...], hi_ref[...], preferred_element_type=F32)
    out_ref[:half, :] = g + jnp.dot(cut_ft[...], lo_ref[...], preferred_element_type=F32)
    out_ref[half:, :] = jnp.broadcast_to(jnp.sum(value, axis=1, keepdims=True), (8, ds))


def pick(dst, src, core):
    groups = 8
    cut = dst.shape[0] // groups
    for g in range(groups):
        dst[g * cut:(g + 1) * cut, :] = src[pl.ds(pl.multiple_of((2 * g + core) * cut, cut), cut), :]


def home_kernel(place_ref, ft_ref, hi_ref, lo_ref, out_ref, cut_ft):
    pick(cut_ft, ft_ref, place_ref[1])
    out_ref[...] = jnp.dot(cut_ft[...], hi_ref[...], preferred_element_type=F32) + jnp.dot(
        cut_ft[...], lo_ref[...], preferred_element_type=F32)


def packed(loss):
    hi = loss.astype(BF16).astype(F32)
    mid = (loss - hi).astype(BF16).astype(F32)
    low = loss - hi - mid
    row = lax.broadcasted_iota(jnp.int32, loss.shape, 0)
    out = jnp.where(row == 0, hi, jnp.where(row == 1, mid, jnp.where(row == 2, low, 0.0)))
    return jnp.concatenate([out, jnp.zeros_like(out)], axis=0).astype(BF16)


def unpacked(rows):
    rows = rows.astype(F32)
    return rows[0:1, :] + rows[1:2, :] + rows[2:3, :]


def cores_kernel(xn, place_ref, home_ref, got_ref, away_ref, keep_ref, *sends):
    half = home_ref.shape[0]
    cut = half // xn
    loss = got_ref[half:, :] + away_ref[half:, :]
    x = place_ref[2]
    at = pl.ds(pl.multiple_of(x * cut, cut), cut)
    keep_ref[:cut, :] = home_ref[at, :] + got_ref[at, :]
    keep_ref[cut:, :] = loss
    rows = packed(loss)
    for k, ref in zip((1, 3, 2), sends):
        at = pl.ds(pl.multiple_of(lax.rem(x + k, xn) * cut, cut), cut)
        ref[:cut, :] = (home_ref[at, :] + got_ref[at, :]).astype(BF16)
        ref[cut:, :] = rows


def rows_kernel(place_ref, keep_ref, p_ref, q_ref, r_ref, mine_ref, across_ref, other_ref, total):
    cut = keep_ref.shape[0] - 8
    half = cut // 2
    total[...] = keep_ref[:cut, :]
    loss = keep_ref[cut:, :]
    for ref in (p_ref, q_ref, r_ref):
        total[...] += ref[:cut, :].astype(F32)
        loss = loss + unpacked(ref[cut:, :])
    y = place_ref[3]
    mine_ref[:half, :] = total[pl.ds(pl.multiple_of(y * half, half), half), :]
    mine_ref[half:, :] = loss
    across_ref[:half, :] = mine_ref[:half, :].astype(BF16)
    across_ref[half:, :] = packed(loss)
    other_ref[:half, :] = total[pl.ds(pl.multiple_of((1 - y) * half, half), half), :]
    other_ref[half:, :] = loss


def plane_kernel(mine_ref, p_ref, q_ref, r_ref, out_ref, loss_ref):
    half = out_ref.shape[0]
    out_ref[...] = mine_ref[:half, :] + p_ref[:half, :] + q_ref[:half, :] + r_ref[:half, :].astype(F32)
    loss = mine_ref[half:, :] + p_ref[half:, :] + q_ref[half:, :] + unpacked(r_ref[half:, :])
    loss_ref[...] = loss[:, :LANES]


def merge(*parts):
    top = functools.reduce(jnp.maximum, [p[0:1, :] for p in parts])
    out = [0.0] * 4
    for p in parts:
        w = jnp.exp2(p[0:1, :] - top)
        out = [out[0] + w * p[1:2, :], out[1] + p[2:3, :], out[2] + w * p[3:4, :], out[3] + p[4:5, :]]
    return jnp.concatenate([top] + out + [jnp.zeros((3, top.shape[1]), F32)], axis=0)


def near_kernel(own_ref, above_ref, below_ref, after_ref, pair_ref, window_ref):
    pair = merge(own_ref[...], above_ref[...])
    pair_ref[...] = pair
    window_ref[...] = merge(pair, below_ref[...])


def per_device(features, proj, student_text, teacher_image, teacher_text):
    rows, feat = features.shape
    dt = teacher_text.shape[1]
    ds = student_text.shape[1]
    zn, yn, xn, cn = (lax.axis_size(a) for a in ("z", Y, "x", "c"))
    images = rows * zn
    batch = images * yn * xn * cn
    texts = rows * yn * xn * cn
    column = rows * yn
    gain = float(teacher_gain / np.sqrt(np.float32(dt)))
    half = feat // cn
    place = jnp.stack([lax.axis_index(a) for a in ("z", "c", "x", "yl")]).astype(jnp.int32)

    swap = lambda v: lax.ppermute(v, "c", flip(cn, 1))
    raw = (features, student_text, teacher_image, teacher_text)
    img = jnp.concatenate([teacher_image, features], axis=1)
    txt = jnp.concatenate([teacher_text, student_text], axis=1)
    txts, imgs, st_own = pl.pallas_call(
        chip_kernel,
        in_specs=[SMEM] + [VMEM] * 6,
        out_specs=[VMEM] * 3,
        out_shape=[shape((rows, dt + ds), BF16), shape((2 * rows, dt + feat), BF16), shape((rows, ds), BF16)],
        compiler_params=params(),
        cost_estimate=FREE,
        name="chip",
    )(place, img, txt, *(swap(v) for v in raw))

    def plane(v, step, stage):
        pairs = []
        dims = (yn // 2, xn, 2, cn)
        for src in np.ndindex(*dims):
            yh, x, yl, c = src
            y = 2 * yh + yl
            if c == stage:
                y = (y + step) % yn
            else:
                x = (x + step) % xn
            dst = (y // 2, x, y % 2, c)
            pairs.append((int(np.ravel_multi_index(src, dims)), int(np.ravel_multi_index(dst, dims))))
        return lax.ppermute(v, ("yh", "x", "yl", "c"), pairs)

    def climb(v, step):
        pairs = [(z * cn + c, (z + (step if c == 0 else -step)) % zn * cn + c) for z in range(zn) for c in range(cn)]
        return lax.ppermute(v, ("z", "c"), pairs)

    together = lax.optimization_barrier
    left, right, far, one, two = together((plane(txts, 1, 0), plane(txts, -1, 0), plane(txts, 2, 0), climb(imgs, 1), climb(imgs, 2)))
    own_col = pl.pallas_call(
        column_kernel,
        in_specs=[VMEM] * 4,
        out_specs=VMEM,
        out_shape=shape((column, dt + ds), BF16),
        compiler_params=params(),
        name="column",
    )(txts, left, right, far)
    left_col, right_col = plane(own_col, 1, 1), plane(own_col, -1, 1)
    far_col = plane(left_col, 1, 1)
    three = climb(one, 2)
    four = climb(two[:rows], 2)
    mine = [one, two, three]
    theirs = [swap(v[rows:]) for v in mine]

    timg, feats, simg, simgb, inv, self_col, diag = pl.pallas_call(
        functools.partial(images_kernel, zn, dt),
        in_specs=[SMEM] + [VMEM] * (4 + 2 * len(mine)),
        out_specs=[VMEM] * 7,
        out_shape=[shape((images, dt), BF16), shape((images, feat), BF16), shape((images, ds), F32), shape((images, ds), BF16),
                   shape((images, LANES), F32), shape((images, LANES), F32), shape((rows, ds), F32)],
        compiler_params=params(),
        cost_estimate=FREE,
        name="images",
    )(place, st_own, proj, imgs, *mine, *theirs, four)

    blocks = [(own_col, swap(own_col)), (left_col, swap(left_col)), (right_col, swap(right_col)), None]
    span = column * cn
    stat = self_col
    chain = []
    stats = []
    for n, block in enumerate(blocks):
        final = n == len(blocks) - 1
        if final:
            block = (far_col, swap(far_col))
        big = [shape((images, texts), BF16)] * 3 + [shape((texts, ds), BF16), shape((images, 5 * LANES), F32), shape((images, LANES), F32)]
        out = pl.pallas_call(
            make_block(n, final, gain, [v.shape[0] for v in block]),
            in_specs=[VMEM] * (3 + len(block) + len(chain)),
            out_specs=[VMEM] * (7 if final else 6),
            out_shape=big + ([shape((8, images), F32)] if final else []),
            scratch_shapes=[pltpu.VMEM((images, span), F32)] * 2,
            input_output_aliases={3 + len(block) + k: k for k in range(len(chain))} | ({2: 4} if n else {}),
            compiler_params=params(),
            cost_estimate=FREE,
            name="block" + str(n),
        )(timg, simgb, stat, *block, *chain)
        chain, stat = list(out[:4]), out[4]
        stats.append(out[5])
        if n == 1:
            far_col, stat = together((far_col, stat))
    flat = out[6]
    te, se, sig, stu = chain

    a, c, ft, done_student = pl.pallas_call(
        student_kernel,
        in_specs=[VMEM] * 6,
        out_specs=[VMEM] * 4,
        out_shape=[shape((images, ds), BF16)] * 2 + [shape((feat, images), BF16), shape((8, LANES), F32)],
        compiler_params=params(),
        cost_estimate=FREE,
        name="student",
    )(se, sig, stu, simg, inv, feats)
    b = pl.pallas_call(
        teacher_kernel,
        in_specs=[VMEM] * (4 + len(stats)),
        out_specs=VMEM,
        out_shape=shape((images, ds), BF16),
        scratch_shapes=[pltpu.VMEM((images, texts), BF16)],
        compiler_params=params(),
        cost_estimate=FREE,
        name="teacher",
    )(te, stu, simg, inv, *stats)

    below = lax.ppermute(flat, "z", ring(zn, 1))
    above = lax.ppermute(flat, "z", ring(zn, zn - 1))
    pair, window = pl.pallas_call(
        near_kernel,
        in_specs=[VMEM] * 4,
        out_specs=[VMEM] * 2,
        out_shape=[shape((8, images), F32)] * 2,
        compiler_params=params(),
        name="near",
    )(flat, above, below, done_student)
    ahead = lax.ppermute(window, "z", ring(zn, zn - 3))
    behind = lax.ppermute(pair, "z", ring(zn, 3))

    away, hi, lo, val = pl.pallas_call(
        away_kernel,
        in_specs=[SMEM] + [VMEM] * 9,
        out_specs=[VMEM] * 4,
        out_shape=[shape((half + 8, ds), F32), shape((images, ds), BF16), shape((images, ds), BF16), shape((8, images), F32)],
        scratch_shapes=[pltpu.VMEM((images, LANES), F32), pltpu.VMEM((half, images), BF16)],
        compiler_params=params(),
        cost_estimate=FREE,
        name="away",
    )(place, window, ahead, behind, flat, a, b, c, diag, ft)
    arrived = swap(away)
    home = pl.pallas_call(
        home_kernel,
        in_specs=[SMEM] + [VMEM] * 3,
        out_specs=VMEM,
        out_shape=shape((half, ds), F32),
        scratch_shapes=[pltpu.VMEM((half, images), BF16)],
        compiler_params=params(),
        cost_estimate=FREE,
        name="home",
    )(place, ft, hi, lo)

    cut = half // xn
    keep, *sends = pl.pallas_call(
        functools.partial(cores_kernel, xn),
        in_specs=[SMEM] + [VMEM] * 3,
        out_specs=[VMEM] * 4,
        out_shape=[shape((cut + 8, ds), F32)] + [shape((cut + 16, ds), BF16)] * 3,
        compiler_params=params(),
        name="cores",
    )(place, home, arrived, away)
    got = [lax.ppermute(v, "x", ring(xn, k)) for k, v in zip((1, 3, 2), sends)]
    cut = cut // 2
    mine, across, other = pl.pallas_call(
        rows_kernel,
        in_specs=[SMEM] + [VMEM] * 4,
        out_specs=[VMEM] * 3,
        out_shape=[shape((cut + 8, ds), F32), shape((cut + 16, ds), BF16), shape((cut + 8, ds), F32)],
        scratch_shapes=[pltpu.VMEM((2 * cut, ds), F32)],
        compiler_params=params(),
        name="rows",
    )(place, keep, *got)
    own, loss = pl.pallas_call(
        plane_kernel,
        in_specs=[VMEM] * 4,
        out_specs=[VMEM] * 2,
        out_shape=[shape((cut, ds), F32), shape((8, LANES), F32)],
        compiler_params=params(),
        name="plane",
    )(mine, lax.ppermute(other, Y, ring(yn, 1)), lax.ppermute(other, Y, ring(yn, 3)), lax.ppermute(across, Y, ring(yn, 2)))

    below = lax.ppermute(own, "z", ring(zn, 1))
    above = lax.ppermute(own, "z", ring(zn, zn - 1))
    pair = own + above
    window = pair + below
    ahead = lax.ppermute(window.astype(BF16), "z", ring(zn, zn - 3))
    behind = lax.ppermute(pair.astype(BF16), "z", ring(zn, 3))
    grad = window + ahead.astype(F32) + behind.astype(F32)

    row_loss = lax.dynamic_slice_in_dim(val[0], lax.axis_index("z") * rows, rows, 0)
    return (row_loss, loss[0, 0] / batch, grad)


def solution(mesh):
    sizes = dict(mesh.shape)
    fine = Mesh(np.asarray(mesh.devices).reshape(sizes["blk"] // 2, 2, sizes["img"] // 4, 2, 2), ALL)
    return jax.shard_map(
        per_device,
        mesh=fine,
        in_specs=(P(ALL, None), P(), P(ALL, None), P(ALL, None), P(ALL, None)),
        out_specs=(P(ALL), P(), P(("x", "yl", "c"), None)),
        check_vma=False,
    )
```

```python
import functools

import jax
import jax.numpy as jnp
import numpy as np
from jax import lax
from jax.experimental import pallas as pl
from jax.experimental.pallas import tpu as pltpu
from jax.sharding import Mesh, PartitionSpec as P

sig_scale = 10.0
sig_bias = -10.0
teacher_gain = 3.0
eps_value = 1e-06

F32 = jnp.float32
BF16 = jnp.bfloat16
LOG2E = float(np.log2(np.e))
LN2 = float(np.log(2.0))
NT = (((1,), (1,)), ((), ()))
ALL = ("z", "yh", "x", "yl", "c")
Y = ("yh", "yl")
VMEM_LIMIT = 8 * 1024 * 1024
FREE = pl.CostEstimate(flops=1, bytes_accessed=1, transcendentals=0)
LANES = 128
STEP = 8
GROUP = 32
PART = 256


def ring(n, k):
    return [(i, (i + k) % n) for i in range(n)]


def flip(n, k):
    return [(i, i ^ k) for i in range(n)]


SMEM = pl.BlockSpec(memory_space=pltpu.SMEM)
VMEM = pl.BlockSpec(memory_space=pltpu.VMEM)


def shape(dims, dtype):
    return jax.ShapeDtypeStruct(dims, dtype)


def params():
    return pltpu.CompilerParams(vmem_limit_bytes=VMEM_LIMIT)


def chip_kernel(place_ref, img_ref, txt_ref, feat2_ref, txt2_ref, timg2_ref, ttxt2_ref, txts_ref, imgs_ref, stxt_ref):
    rows, dt = ttxt2_ref.shape
    half = rows // 2
    mine = pl.ds(pl.multiple_of(place_ref[1] * half, half), half)
    stxt_ref[...] = unit(txt_ref[:, dt:])
    txts_ref[:half, :dt] = txt_ref[mine, :dt]
    txts_ref[half:, :dt] = ttxt2_ref[mine, :]
    txts_ref[:half, dt:] = stxt_ref[mine, :]
    txts_ref[half:, dt:] = unit(txt2_ref[mine, :])
    imgs_ref[:rows, :] = img_ref[...]
    imgs_ref[rows:, :dt] = timg2_ref[...]
    imgs_ref[rows:, dt:] = feat2_ref[...]


def unit(txt):
    txt = txt.astype(F32)
    return (txt / jnp.sqrt(jnp.sum(txt * txt, axis=1, keepdims=True) + eps_value)).astype(BF16)


def column_kernel(a_ref, b_ref, c_ref, d_ref, out_ref):
    rows = a_ref.shape[0]
    for n, ref in enumerate((a_ref, b_ref, c_ref, d_ref)):
        out_ref[n * rows:(n + 1) * rows, :] = ref[...]


def images_kernel(zn, dt, place_ref, own_txt_ref, proj_ref, *refs):
    count = zn // 2 - 1
    img_ref, mine, theirs, last_ref = refs[0], refs[1:1 + count], refs[1 + count:1 + 2 * count], refs[1 + 2 * count]
    timg_ref, feat_ref, simg_ref, simgb_ref, inv_ref, self_ref, diag_ref = refs[2 + 2 * count:]
    rows = img_ref.shape[0] // 2
    z = place_ref[0]
    side = 1 - 2 * place_ref[1]

    def put(ref, shift):
        at = pl.ds(pl.multiple_of(lax.rem(z + shift + zn, zn) * rows, rows), rows)
        timg_ref[at, :] = ref[:rows, :dt]
        feat_ref[at, :] = ref[:rows, dt:]

    put(img_ref, 0)
    for k in range(count):
        put(mine[k], -side * (k + 1))
        put(theirs[k], side * (k + 1))
    put(last_ref, zn // 2)

    def part(p, none):
        some = pl.ds(pl.multiple_of(p * PART, PART), PART)
        pre = jnp.dot(feat_ref[some, :], proj_ref[...], preferred_element_type=F32)
        norm = jnp.sqrt(jnp.sum(pre * pre, axis=1, keepdims=True) + eps_value)
        simg = pre / norm
        simg_ref[some, :] = simg
        simgb_ref[some, :] = simg.astype(BF16)
        inv_ref[some, :] = jnp.broadcast_to(1.0 / norm, (PART, LANES))
        return none

    lax.fori_loop(0, simg_ref.shape[0] // PART, part, 0)
    own = pl.ds(pl.multiple_of(z * rows, rows), rows)
    s = simg_ref[own, :]
    txt = own_txt_ref[...].astype(F32)
    margin = sig_scale * jnp.sum(s.astype(BF16).astype(F32) * txt, axis=1, keepdims=True) + sig_bias
    self_ref[...] = jnp.zeros_like(self_ref)
    lane = lax.broadcasted_iota(jnp.int32, (rows, LANES), 1)
    self_ref[own, :] = jnp.where(lane == 0, -margin, 0.0)
    d = -sig_scale * txt
    diag_ref[...] = (d - s * jnp.sum(s * d, axis=1, keepdims=True)) * inv_ref[own, 0:1]


def make_block(index, last, gain, sizes):
    first = index == 0
    span = sum(sizes)

    def kernel(timg_ref, simgb_ref, old_ref, *refs):
        texts, refs = refs[:len(sizes)], refs[len(sizes):]
        if not first:
            refs = refs[4:]
        te_ref, se_ref, sig_ref, stu_ref, stat_ref, top_ref = refs[:6]
        flat_ref = refs[6] if last else None
        tl, sl = refs[-2:]
        dt = timg_ref.shape[1]
        images = timg_ref.shape[0]
        cols = slice(index * span, (index + 1) * span)
        shrink = float(np.exp(sig_bias))
        fold = lambda v: sum((v[:, k:k + LANES] for k in range(LANES, span, LANES)), v[:, :LANES])
        at = 0
        for ref, n in zip(texts, sizes):
            stu_ref[index * span + at:index * span + at + n, :] = ref[:, dt:]
            at += n
        def part(p, none):
            rows = pl.ds(pl.multiple_of(p * PART, PART), PART)
            at = 0
            for ref, n in zip(texts, sizes):
                tl[rows, at:at + n] = lax.dot_general(timg_ref[rows, :], ref[:, :dt], NT, preferred_element_type=F32)
                sl[rows, at:at + n] = lax.dot_general(simgb_ref[rows, :], ref[:, dt:], NT, preferred_element_type=F32)
                at += n
            return none

        lax.fori_loop(0, images // PART, part, 0)

        def body(k, none):
            for u in range(0, GROUP, 2 * STEP):
                at = pl.multiple_of(k * GROUP + u, 2 * STEP)
                outs = []
                for half in range(2):
                    rows = pl.ds(pl.multiple_of(at + half * STEP, STEP), STEP)
                    t = (gain * LOG2E) * tl[rows, :]
                    s = (sig_scale * LOG2E) * sl[rows, :]
                    top = jnp.max(t, axis=1, keepdims=True)
                    if not first:
                        top = jnp.maximum(top, old_ref[rows, :LANES])
                    top = jnp.broadcast_to(top, (STEP, LANES))
                    te = jnp.exp2(t - jnp.concatenate([top] * (span // LANES), axis=1))
                    se = jnp.exp2(s)
                    em = se * shrink
                    up = 1.0 + em
                    sig = em * pl.reciprocal(up, approx=True)
                    soft = jnp.log(up) + (em - (up - 1.0))
                    outs.append((te, se, sig))
                    sums = [fold(te), fold(se), fold(te * (t - s)), fold(soft)]
                    if first:
                        sums[3] = sums[3] + old_ref[rows, :]
                    else:
                        w = jnp.exp2(old_ref[rows, :LANES] - top)
                        was = [old_ref[rows, j * LANES:(j + 1) * LANES] for j in range(1, 5)]
                        sums = [sums[0] + w * was[0], sums[1] + was[1], sums[2] + w * was[2], sums[3] + was[3]]
                    top_ref[rows, :] = top
                    for j, v in enumerate([top] + sums):
                        stat_ref[rows, j * LANES:(j + 1) * LANES] = v
                for ref, low, high in zip((te_ref, se_ref, sig_ref), *outs):
                    ref[pl.ds(at, 2 * STEP), cols] = jnp.concatenate([low, high], axis=0).astype(BF16)
            return none

        lax.fori_loop(0, images // GROUP, body, 0)
        if last:
            ones = jnp.ones((8, LANES), F32)
            out = [stat_ref[:, :LANES].T[:1, :]]
            for k in range(1, 5):
                v = lax.dot_general(ones, stat_ref[:, k * LANES:(k + 1) * LANES], NT, precision=lax.Precision.HIGHEST, preferred_element_type=F32)
                out.append(v[:1, :])
            flat_ref[...] = jnp.concatenate(out + [jnp.zeros((3, images), F32)], axis=0)

    return kernel


def carry(weights, txt, simg, inv):
    d = jnp.dot(weights, txt, preferred_element_type=F32)
    along = jnp.sum(simg * d, axis=1, keepdims=True)
    return ((d - simg * along) * inv).astype(BF16)


def student_kernel(se_ref, sig_ref, stu_ref, simg_ref, inv_ref, feat_ref, a_ref, c_ref, ft_ref, done_ref):
    def part(p, none):
        rows = pl.ds(pl.multiple_of(p * PART, PART), PART)
        for src, dst in ((se_ref, a_ref), (sig_ref, c_ref)):
            dst[rows, :] = carry(src[rows, :], stu_ref[...], simg_ref[rows, :], inv_ref[rows, 0:1])
        return none

    lax.fori_loop(0, se_ref.shape[0] // PART, part, 0)
    ft_ref[...] = feat_ref[...].T
    done_ref[...] = jnp.zeros_like(done_ref)


def teacher_kernel(te_ref, stu_ref, simg_ref, inv_ref, *refs):
    stats, (b_ref, scaled) = refs[:-2], refs[-2:]
    span = te_ref.shape[1] // len(stats)

    def part(p, none):
        rows = pl.ds(pl.multiple_of(p * PART, PART), PART)
        top = stats[-1][rows, 0:1]
        for n, stat in enumerate(stats):
            cols = slice(n * span, (n + 1) * span)
            w = jnp.exp2(stat[rows, 0:1] - top)
            scaled[rows, cols] = (te_ref[rows, cols].astype(F32) * w).astype(BF16)
        b_ref[rows, :] = carry(scaled[rows, :], stu_ref[...], simg_ref[rows, :], inv_ref[rows, 0:1])
        return none

    lax.fori_loop(0, te_ref.shape[0] // PART, part, 0)


def away_kernel(place_ref, window_ref, ahead_ref, behind_ref, flat_ref, a_ref, b_ref, c_ref, diag_ref, ft_ref,
                out_ref, hi_ref, lo_ref, val_ref, turned, cut_ft):
    rows = diag_ref.shape[0]
    half, ds = cut_ft.shape[0], a_ref.shape[1]
    sums = merge(window_ref[...], ahead_ref[...], behind_ref[...])
    top, tsum, ssum, tval, soft = (sums[k:k + 1, :] for k in range(5))
    value = tval / tsum * LN2 + soft - (top * LN2 + jnp.log(tsum)) + jnp.log(ssum)
    val_ref[...] = jnp.broadcast_to(value, val_ref.shape)
    ca = sig_scale / ssum
    cb = -sig_scale * jnp.exp2(flat_ref[0:1, :] - top) / tsum
    row = lax.broadcasted_iota(jnp.int32, (LANES, ca.shape[1]), 0)
    turned[...] = jnp.where(row == 0, ca, cb).T

    def part(p, none):
        some = pl.ds(pl.multiple_of(p * LANES, LANES), LANES)
        d = turned[some, 0:1] * a_ref[some, :].astype(F32) + turned[some, 1:2] * b_ref[some, :].astype(F32)
        d = d + sig_scale * c_ref[some, :].astype(F32)
        hi = d.astype(BF16)
        hi_ref[some, :] = hi
        lo_ref[some, :] = (d - hi.astype(F32)).astype(BF16)
        return none

    lax.fori_loop(0, hi_ref.shape[0] // LANES, part, 0)
    own = pl.ds(pl.multiple_of(place_ref[0] * rows, rows), rows)
    mine = hi_ref[own, :].astype(F32) + lo_ref[own, :].astype(F32) + diag_ref[...]
    mine_hi = mine.astype(BF16)
    hi_ref[own, :] = mine_hi
    lo_ref[own, :] = (mine - mine_hi.astype(F32)).astype(BF16)
    pick(cut_ft, ft_ref, 1 - place_ref[1])
    g = jnp.dot(cut_ft[...], hi_ref[...], preferred_element_type=F32)
    out_ref[:half, :] = g + jnp.dot(cut_ft[...], lo_ref[...], preferred_element_type=F32)
    out_ref[half:, :] = jnp.broadcast_to(jnp.sum(value, axis=1, keepdims=True), (8, ds))


def pick(dst, src, core):
    groups = 8
    cut = dst.shape[0] // groups
    for g in range(groups):
        dst[g * cut:(g + 1) * cut, :] = src[pl.ds(pl.multiple_of((2 * g + core) * cut, cut), cut), :]


def home_kernel(place_ref, ft_ref, hi_ref, lo_ref, out_ref, cut_ft):
    pick(cut_ft, ft_ref, place_ref[1])
    out_ref[...] = jnp.dot(cut_ft[...], hi_ref[...], preferred_element_type=F32) + jnp.dot(
        cut_ft[...], lo_ref[...], preferred_element_type=F32)


def packed(loss):
    hi = loss.astype(BF16).astype(F32)
    mid = (loss - hi).astype(BF16).astype(F32)
    low = loss - hi - mid
    row = lax.broadcasted_iota(jnp.int32, loss.shape, 0)
    out = jnp.where(row == 0, hi, jnp.where(row == 1, mid, jnp.where(row == 2, low, 0.0)))
    return jnp.concatenate([out, jnp.zeros_like(out)], axis=0).astype(BF16)


def unpacked(rows):
    rows = rows.astype(F32)
    return rows[0:1, :] + rows[1:2, :] + rows[2:3, :]


def cores_kernel(xn, place_ref, home_ref, got_ref, away_ref, keep_ref, *sends):
    half = home_ref.shape[0]
    cut = half // xn
    loss = got_ref[half:, :] + away_ref[half:, :]
    x = place_ref[2]
    at = pl.ds(pl.multiple_of(x * cut, cut), cut)
    keep_ref[:cut, :] = home_ref[at, :] + got_ref[at, :]
    keep_ref[cut:, :] = loss
    rows = packed(loss)
    for k, ref in zip((1, 3, 2), sends):
        at = pl.ds(pl.multiple_of(lax.rem(x + k, xn) * cut, cut), cut)
        ref[:cut, :] = (home_ref[at, :] + got_ref[at, :]).astype(BF16)
        ref[cut:, :] = rows


def rows_kernel(place_ref, keep_ref, p_ref, q_ref, r_ref, mine_ref, across_ref, other_ref, total):
    cut = keep_ref.shape[0] - 8
    half = cut // 2
    total[...] = keep_ref[:cut, :]
    loss = keep_ref[cut:, :]
    for ref in (p_ref, q_ref, r_ref):
        total[...] += ref[:cut, :].astype(F32)
        loss = loss + unpacked(ref[cut:, :])
    y = place_ref[3]
    mine_ref[:half, :] = total[pl.ds(pl.multiple_of(y * half, half), half), :]
    mine_ref[half:, :] = loss
    across_ref[:half, :] = mine_ref[:half, :].astype(BF16)
    across_ref[half:, :] = packed(loss)
    other_ref[:half, :] = total[pl.ds(pl.multiple_of((1 - y) * half, half), half), :]
    other_ref[half:, :] = loss


def plane_kernel(mine_ref, p_ref, q_ref, r_ref, out_ref, loss_ref):
    half = out_ref.shape[0]
    out_ref[...] = mine_ref[:half, :] + p_ref[:half, :] + q_ref[:half, :] + r_ref[:half, :].astype(F32)
    loss = mine_ref[half:, :] + p_ref[half:, :] + q_ref[half:, :] + unpacked(r_ref[half:, :])
    loss_ref[...] = loss[:, :LANES]


def merge(*parts):
    top = functools.reduce(jnp.maximum, [p[0:1, :] for p in parts])
    out = [0.0] * 4
    for p in parts:
        w = jnp.exp2(p[0:1, :] - top)
        out = [out[0] + w * p[1:2, :], out[1] + p[2:3, :], out[2] + w * p[3:4, :], out[3] + p[4:5, :]]
    return jnp.concatenate([top] + out + [jnp.zeros((3, top.shape[1]), F32)], axis=0)


def near_kernel(own_ref, above_ref, below_ref, after_ref, pair_ref, window_ref):
    pair = merge(own_ref[...], above_ref[...])
    pair_ref[...] = pair
    window_ref[...] = merge(pair, below_ref[...])


def per_device(features, proj, student_text, teacher_image, teacher_text):
    rows, feat = features.shape
    dt = teacher_text.shape[1]
    ds = student_text.shape[1]
    zn, yn, xn, cn = (lax.axis_size(a) for a in ("z", Y, "x", "c"))
    images = rows * zn
    batch = images * yn * xn * cn
    texts = rows * yn * xn * cn
    column = rows * yn
    gain = float(teacher_gain / np.sqrt(np.float32(dt)))
    half = feat // cn
    place = jnp.stack([lax.axis_index(a) for a in ("z", "c", "x", "yl")]).astype(jnp.int32)

    swap = lambda v: lax.ppermute(v, "c", flip(cn, 1))
    raw = (features, student_text, teacher_image, teacher_text)
    img = jnp.concatenate([teacher_image, features], axis=1)
    txt = jnp.concatenate([teacher_text, student_text], axis=1)
    txts, imgs, st_own = pl.pallas_call(
        chip_kernel,
        in_specs=[SMEM] + [VMEM] * 6,
        out_specs=[VMEM] * 3,
        out_shape=[shape((rows, dt + ds), BF16), shape((2 * rows, dt + feat), BF16), shape((rows, ds), BF16)],
        compiler_params=params(),
        cost_estimate=FREE,
        name="chip",
    )(place, img, txt, *(swap(v) for v in raw))

    def plane(v, step, stage):
        pairs = []
        dims = (yn // 2, xn, 2, cn)
        for src in np.ndindex(*dims):
            yh, x, yl, c = src
            y = 2 * yh + yl
            if c == stage:
                y = (y + step) % yn
            else:
                x = (x + step) % xn
            dst = (y // 2, x, y % 2, c)
            pairs.append((int(np.ravel_multi_index(src, dims)), int(np.ravel_multi_index(dst, dims))))
        return lax.ppermute(v, ("yh", "x", "yl", "c"), pairs)

    def climb(v, step):
        pairs = [(z * cn + c, (z + (step if c == 0 else -step)) % zn * cn + c) for z in range(zn) for c in range(cn)]
        return lax.ppermute(v, ("z", "c"), pairs)

    together = lax.optimization_barrier
    left, right, far, one, two = together((plane(txts, 1, 0), plane(txts, -1, 0), plane(txts, 2, 0), climb(imgs, 1), climb(imgs, 2)))
    own_col = pl.pallas_call(
        column_kernel,
        in_specs=[VMEM] * 4,
        out_specs=VMEM,
        out_shape=shape((column, dt + ds), BF16),
        compiler_params=params(),
        name="column",
    )(txts, left, right, far)
    left_col, right_col = plane(own_col, 1, 1), plane(own_col, -1, 1)
    far_col = plane(left_col, 1, 1)
    three = climb(one, 2)
    four = climb(two[:rows], 2)
    mine = [one, two, three]
    theirs = [swap(v[rows:]) for v in mine]

    timg, feats, simg, simgb, inv, self_col, diag = pl.pallas_call(
        functools.partial(images_kernel, zn, dt),
        in_specs=[SMEM] + [VMEM] * (4 + 2 * len(mine)),
        out_specs=[VMEM] * 7,
        out_shape=[shape((images, dt), BF16), shape((images, feat), BF16), shape((images, ds), F32), shape((images, ds), BF16),
                   shape((images, LANES), F32), shape((images, LANES), F32), shape((rows, ds), F32)],
        compiler_params=params(),
        cost_estimate=FREE,
        name="images",
    )(place, st_own, proj, imgs, *mine, *theirs, four)

    blocks = [(own_col, swap(own_col)), (left_col, swap(left_col)), (right_col, swap(right_col)), None]
    span = column * cn
    stat = self_col
    chain = []
    stats = []
    for n, block in enumerate(blocks):
        final = n == len(blocks) - 1
        if final:
            block = (far_col, swap(far_col))
        big = [shape((images, texts), BF16)] * 3 + [shape((texts, ds), BF16), shape((images, 5 * LANES), F32), shape((images, LANES), F32)]
        out = pl.pallas_call(
            make_block(n, final, gain, [v.shape[0] for v in block]),
            in_specs=[VMEM] * (3 + len(block) + len(chain)),
            out_specs=[VMEM] * (7 if final else 6),
            out_shape=big + ([shape((8, images), F32)] if final else []),
            scratch_shapes=[pltpu.VMEM((images, span), F32)] * 2,
            input_output_aliases={3 + len(block) + k: k for k in range(len(chain))} | ({2: 4} if n else {}),
            compiler_params=params(),
            cost_estimate=FREE,
            name="block" + str(n),
        )(timg, simgb, stat, *block, *chain)
        chain, stat = list(out[:4]), out[4]
        stats.append(out[5])
        if n == 1:
            far_col, stat = together((far_col, stat))
    flat = out[6]
    te, se, sig, stu = chain

    a, c, ft, done_student = pl.pallas_call(
        student_kernel,
        in_specs=[VMEM] * 6,
        out_specs=[VMEM] * 4,
        out_shape=[shape((images, ds), BF16)] * 2 + [shape((feat, images), BF16), shape((8, LANES), F32)],
        compiler_params=params(),
        cost_estimate=FREE,
        name="student",
    )(se, sig, stu, simg, inv, feats)
    b = pl.pallas_call(
        teacher_kernel,
        in_specs=[VMEM] * (4 + len(stats)),
        out_specs=VMEM,
        out_shape=shape((images, ds), BF16),
        scratch_shapes=[pltpu.VMEM((images, texts), BF16)],
        compiler_params=params(),
        cost_estimate=FREE,
        name="teacher",
    )(te, stu, simg, inv, *stats)

    below = lax.ppermute(flat, "z", ring(zn, 1))
    above = lax.ppermute(flat, "z", ring(zn, zn - 1))
    pair, window = pl.pallas_call(
        near_kernel,
        in_specs=[VMEM] * 4,
        out_specs=[VMEM] * 2,
        out_shape=[shape((8, images), F32)] * 2,
        compiler_params=params(),
        name="near",
    )(flat, above, below, done_student)
    ahead = lax.ppermute(window, "z", ring(zn, zn - 3))
    behind = lax.ppermute(pair, "z", ring(zn, 3))

    away, hi, lo, val = pl.pallas_call(
        away_kernel,
        in_specs=[SMEM] + [VMEM] * 9,
        out_specs=[VMEM] * 4,
        out_shape=[shape((half + 8, ds), F32), shape((images, ds), BF16), shape((images, ds), BF16), shape((8, images), F32)],
        scratch_shapes=[pltpu.VMEM((images, LANES), F32), pltpu.VMEM((half, images), BF16)],
        compiler_params=params(),
        cost_estimate=FREE,
        name="away",
    )(place, window, ahead, behind, flat, a, b, c, diag, ft)
    arrived = swap(away)
    home = pl.pallas_call(
        home_kernel,
        in_specs=[SMEM] + [VMEM] * 3,
        out_specs=VMEM,
        out_shape=shape((half, ds), F32),
        scratch_shapes=[pltpu.VMEM((half, images), BF16)],
        compiler_params=params(),
        cost_estimate=FREE,
        name="home",
    )(place, ft, hi, lo)

    cut = half // xn
    keep, *sends = pl.pallas_call(
        functools.partial(cores_kernel, xn),
        in_specs=[SMEM] + [VMEM] * 3,
        out_specs=[VMEM] * 4,
        out_shape=[shape((cut + 8, ds), F32)] + [shape((cut + 16, ds), BF16)] * 3,
        compiler_params=params(),
        name="cores",
    )(place, home, arrived, away)
    got = [lax.ppermute(v, "x", ring(xn, k)) for k, v in zip((1, 3, 2), sends)]
    cut = cut // 2
    mine, across, other = pl.pallas_call(
        rows_kernel,
        in_specs=[SMEM] + [VMEM] * 4,
        out_specs=[VMEM] * 3,
        out_shape=[shape((cut + 8, ds), F32), shape((cut + 16, ds), BF16), shape((cut + 8, ds), F32)],
        scratch_shapes=[pltpu.VMEM((2 * cut, ds), F32)],
        compiler_params=params(),
        name="rows",
    )(place, keep, *got)
    own, loss = pl.pallas_call(
        plane_kernel,
        in_specs=[VMEM] * 4,
        out_specs=[VMEM] * 2,
        out_shape=[shape((cut, ds), F32), shape((8, LANES), F32)],
        compiler_params=params(),
        name="plane",
    )(mine, lax.ppermute(other, Y, ring(yn, 1)), lax.ppermute(other, Y, ring(yn, 3)), lax.ppermute(across, Y, ring(yn, 2)))

    below = lax.ppermute(own, "z", ring(zn, 1))
    above = lax.ppermute(own, "z", ring(zn, zn - 1))
    pair = own + above
    window = pair + below
    ahead = lax.ppermute(window.astype(BF16), "z", ring(zn, zn - 3))
    behind = lax.ppermute(pair.astype(BF16), "z", ring(zn, 3))
    grad = window + ahead.astype(F32) + behind.astype(F32)

    row_loss = lax.dynamic_slice_in_dim(val[0], lax.axis_index("z") * rows, rows, 0)
    return (row_loss, loss[0, 0] / batch, grad)


def solution(mesh):
    sizes = dict(mesh.shape)
    fine = Mesh(np.asarray(mesh.devices).reshape(sizes["blk"] // 2, 2, sizes["img"] // 4, 2, 2), ALL)
    return jax.shard_map(
        per_device,
        mesh=fine,
        in_specs=(P(ALL, None), P(), P(ALL, None), P(ALL, None), P(ALL, None)),
        out_specs=(P(ALL), P(), P(("x", "yl", "c"), None)),
        check_vma=False,
    )
```

```python
import functools

import jax
import jax.numpy as jnp
import numpy as np
from jax import lax
from jax.experimental import pallas as pl
from jax.experimental.pallas import tpu as pltpu
from jax.sharding import Mesh, PartitionSpec as P

sig_scale = 10.0
sig_bias = -10.0
teacher_gain = 3.0
eps_value = 1e-06

F32 = jnp.float32
BF16 = jnp.bfloat16
LOG2E = float(np.log2(np.e))
LN2 = float(np.log(2.0))
NT = (((1,), (1,)), ((), ()))
ALL = ("z", "yh", "x", "yl", "c")
Y = ("yh", "yl")
VMEM_LIMIT = 8 * 1024 * 1024
FREE = pl.CostEstimate(flops=1, bytes_accessed=1, transcendentals=0)
LANES = 128
STEP = 8
GROUP = 128
PART = 256


def ring(n, k):
    return [(i, (i + k) % n) for i in range(n)]


def flip(n, k):
    return [(i, i ^ k) for i in range(n)]


SMEM = pl.BlockSpec(memory_space=pltpu.SMEM)
VMEM = pl.BlockSpec(memory_space=pltpu.VMEM)


def shape(dims, dtype):
    return jax.ShapeDtypeStruct(dims, dtype)


def params():
    return pltpu.CompilerParams(vmem_limit_bytes=VMEM_LIMIT)


def chip_kernel(place_ref, img_ref, txt_ref, feat2_ref, txt2_ref, timg2_ref, ttxt2_ref, txts_ref, imgs_ref, stxt_ref):
    rows, dt = ttxt2_ref.shape
    half = rows // 2
    mine = pl.ds(pl.multiple_of(place_ref[1] * half, half), half)
    stxt_ref[...] = unit(txt_ref[:, dt:])
    txts_ref[:half, :dt] = txt_ref[mine, :dt]
    txts_ref[half:, :dt] = ttxt2_ref[mine, :]
    txts_ref[:half, dt:] = stxt_ref[mine, :]
    txts_ref[half:, dt:] = unit(txt2_ref[mine, :])
    imgs_ref[:rows, :] = img_ref[...]
    imgs_ref[rows:, :dt] = timg2_ref[...]
    imgs_ref[rows:, dt:] = feat2_ref[...]


def unit(txt):
    txt = txt.astype(F32)
    return (txt / jnp.sqrt(jnp.sum(txt * txt, axis=1, keepdims=True) + eps_value)).astype(BF16)


def onward_kernel(one_ref, two_ref, on_ref, across_ref):
    rows = one_ref.shape[0] // 2
    on_ref[:2 * rows, :] = one_ref[...]
    on_ref[2 * rows:, :] = two_ref[:rows, :]
    across_ref[:rows, :] = one_ref[rows:, :]
    across_ref[rows:, :] = two_ref[rows:, :]


def column_kernel(a_ref, b_ref, c_ref, d_ref, out_ref):
    rows = a_ref.shape[0]
    for n, ref in enumerate((a_ref, b_ref, c_ref, d_ref)):
        out_ref[n * rows:(n + 1) * rows, :] = ref[...]


def images_kernel(zn, dt, place_ref, own_txt_ref, proj_ref, *refs):
    img_ref, one_ref, two_ref, ahead_ref, near_ref, third_ref = refs[:6]
    timg_ref, feat_ref, simg_ref, simgb_ref, inv_ref, self_ref, diag_ref = refs[6:]
    rows = img_ref.shape[0] // 2
    z = place_ref[0]
    side = 1 - 2 * place_ref[1]

    def put(ref, k, shift):
        at = pl.ds(pl.multiple_of(lax.rem(z + shift + zn, zn) * rows, rows), rows)
        timg_ref[at, :] = ref[k * rows:(k + 1) * rows, :dt]
        feat_ref[at, :] = ref[k * rows:(k + 1) * rows, dt:]

    put(img_ref, 0, 0)
    put(one_ref, 0, -side)
    put(two_ref, 0, -2 * side)
    put(ahead_ref, 0, -3 * side)
    put(ahead_ref, 2, zn // 2)
    put(near_ref, 0, side)
    put(near_ref, 1, 2 * side)
    put(third_ref, 0, 3 * side)

    def part(p, none):
        some = pl.ds(pl.multiple_of(p * PART, PART), PART)
        pre = jnp.dot(feat_ref[some, :], proj_ref[...], preferred_element_type=F32)
        norm = jnp.sqrt(jnp.sum(pre * pre, axis=1, keepdims=True) + eps_value)
        simg = pre / norm
        simg_ref[some, :] = simg
        simgb_ref[some, :] = simg.astype(BF16)
        inv_ref[some, :] = jnp.broadcast_to(1.0 / norm, (PART, LANES))
        return none

    lax.fori_loop(0, simg_ref.shape[0] // PART, part, 0)
    own = pl.ds(pl.multiple_of(z * rows, rows), rows)
    s = simg_ref[own, :]
    txt = own_txt_ref[...].astype(F32)
    margin = sig_scale * jnp.sum(s.astype(BF16).astype(F32) * txt, axis=1, keepdims=True) + sig_bias
    self_ref[...] = jnp.zeros_like(self_ref)
    lane = lax.broadcasted_iota(jnp.int32, (rows, LANES), 1)
    self_ref[own, :] = jnp.where(lane == 0, -margin, 0.0)
    d = -sig_scale * txt
    diag_ref[...] = (d - s * jnp.sum(s * d, axis=1, keepdims=True)) * inv_ref[own, 0:1]


def make_block(index, last, gain, sizes):
    first = index == 0
    span = sum(sizes)

    def kernel(timg_ref, simgb_ref, old_ref, *refs):
        texts, refs = refs[:len(sizes)], refs[len(sizes):]
        if not first:
            refs = refs[4:]
        te_ref, se_ref, sig_ref, stu_ref, stat_ref, top_ref = refs[:6]
        flat_ref = refs[6] if last else None
        tl, sl = refs[-2:]
        dt = timg_ref.shape[1]
        images = timg_ref.shape[0]
        cols = slice(index * span, (index + 1) * span)
        shrink = float(np.exp(sig_bias))
        fold = lambda v: sum((v[:, k:k + LANES] for k in range(LANES, span, LANES)), v[:, :LANES])
        at = 0
        for ref, n in zip(texts, sizes):
            stu_ref[index * span + at:index * span + at + n, :] = ref[:, dt:]
            at += n
        at = 0
        for ref, n in zip(texts, sizes):
            tl[:, at:at + n] = lax.dot_general(timg_ref[...], ref[:, :dt], NT, preferred_element_type=F32)
            sl[:, at:at + n] = lax.dot_general(simgb_ref[...], ref[:, dt:], NT, preferred_element_type=F32)
            at += n

        def body(k, none):
            for u in range(0, GROUP, 2 * STEP):
                at = pl.multiple_of(k * GROUP + u, 2 * STEP)
                outs = []
                for half in range(2):
                    rows = pl.ds(pl.multiple_of(at + half * STEP, STEP), STEP)
                    t = (gain * LOG2E) * tl[rows, :]
                    s = (sig_scale * LOG2E) * sl[rows, :]
                    top = jnp.max(t, axis=1, keepdims=True)
                    if not first:
                        top = jnp.maximum(top, old_ref[rows, :LANES])
                    top = jnp.broadcast_to(top, (STEP, LANES))
                    te = jnp.exp2(t - jnp.concatenate([top] * (span // LANES), axis=1))
                    se = jnp.exp2(s)
                    em = se * shrink
                    up = 1.0 + em
                    sig = em * pl.reciprocal(up, approx=True)
                    soft = jnp.log(up) + (em - (up - 1.0))
                    outs.append((te, se, sig))
                    sums = [fold(te), fold(se), fold(te * (t - s)), fold(soft)]
                    if first:
                        sums[3] = sums[3] + old_ref[rows, :]
                    else:
                        w = jnp.exp2(old_ref[rows, :LANES] - top)
                        was = [old_ref[rows, j * LANES:(j + 1) * LANES] for j in range(1, 5)]
                        sums = [sums[0] + w * was[0], sums[1] + was[1], sums[2] + w * was[2], sums[3] + was[3]]
                    top_ref[rows, :] = top
                    for j, v in enumerate([top] + sums):
                        stat_ref[rows, j * LANES:(j + 1) * LANES] = v
                for ref, low, high in zip((te_ref, se_ref, sig_ref), *outs):
                    ref[pl.ds(at, 2 * STEP), cols] = jnp.concatenate([low, high], axis=0).astype(BF16)
            return none

        lax.fori_loop(0, images // GROUP, body, 0)
        if last:
            ones = jnp.ones((8, LANES), F32)
            out = [stat_ref[:, :LANES].T[:1, :]]
            for k in range(1, 5):
                v = lax.dot_general(ones, stat_ref[:, k * LANES:(k + 1) * LANES], NT, precision=lax.Precision.HIGHEST, preferred_element_type=F32)
                out.append(v[:1, :])
            flat_ref[...] = jnp.concatenate(out + [jnp.zeros((3, images), F32)], axis=0)

    return kernel


def carry(weights, txt, simg, inv):
    d = jnp.dot(weights, txt, preferred_element_type=F32)
    along = jnp.sum(simg * d, axis=1, keepdims=True)
    return ((d - simg * along) * inv).astype(BF16)


def student_kernel(se_ref, sig_ref, stu_ref, simg_ref, inv_ref, feat_ref, a_ref, c_ref, ft_ref, done_ref):
    def part(p, none):
        rows = pl.ds(pl.multiple_of(p * PART, PART), PART)
        for src, dst in ((se_ref, a_ref), (sig_ref, c_ref)):
            dst[rows, :] = carry(src[rows, :], stu_ref[...], simg_ref[rows, :], inv_ref[rows, 0:1])
        return none

    lax.fori_loop(0, se_ref.shape[0] // PART, part, 0)
    ft_ref[...] = feat_ref[...].T
    done_ref[...] = jnp.zeros_like(done_ref)


def teacher_kernel(te_ref, stu_ref, simg_ref, inv_ref, *refs):
    stats, (b_ref, scaled) = refs[:-2], refs[-2:]
    span = te_ref.shape[1] // len(stats)

    def part(p, none):
        rows = pl.ds(pl.multiple_of(p * PART, PART), PART)
        top = stats[-1][rows, 0:1]
        for n, stat in enumerate(stats):
            cols = slice(n * span, (n + 1) * span)
            w = jnp.exp2(stat[rows, 0:1] - top)
            scaled[rows, cols] = (te_ref[rows, cols].astype(F32) * w).astype(BF16)
        b_ref[rows, :] = carry(scaled[rows, :], stu_ref[...], simg_ref[rows, :], inv_ref[rows, 0:1])
        return none

    lax.fori_loop(0, te_ref.shape[0] // PART, part, 0)


def away_kernel(place_ref, window_ref, ahead_ref, behind_ref, flat_ref, a_ref, b_ref, c_ref, diag_ref, ft_ref,
                out_ref, hi_ref, lo_ref, val_ref, turned, cut_ft):
    rows = diag_ref.shape[0]
    half, ds = cut_ft.shape[0], a_ref.shape[1]
    sums = merge(window_ref[...], ahead_ref[...], behind_ref[...])
    top, tsum, ssum, tval, soft = (sums[k:k + 1, :] for k in range(5))
    value = tval / tsum * LN2 + soft - (top * LN2 + jnp.log(tsum)) + jnp.log(ssum)
    val_ref[...] = jnp.broadcast_to(value, val_ref.shape)
    ca = sig_scale / ssum
    cb = -sig_scale * jnp.exp2(flat_ref[0:1, :] - top) / tsum
    row = lax.broadcasted_iota(jnp.int32, (LANES, ca.shape[1]), 0)
    turned[...] = jnp.where(row == 0, ca, cb).T

    def part(p, none):
        some = pl.ds(pl.multiple_of(p * LANES, LANES), LANES)
        d = turned[some, 0:1] * a_ref[some, :].astype(F32) + turned[some, 1:2] * b_ref[some, :].astype(F32)
        d = d + sig_scale * c_ref[some, :].astype(F32)
        hi = d.astype(BF16)
        hi_ref[some, :] = hi
        lo_ref[some, :] = (d - hi.astype(F32)).astype(BF16)
        return none

    lax.fori_loop(0, hi_ref.shape[0] // LANES, part, 0)
    own = pl.ds(pl.multiple_of(place_ref[0] * rows, rows), rows)
    mine = hi_ref[own, :].astype(F32) + lo_ref[own, :].astype(F32) + diag_ref[...]
    mine_hi = mine.astype(BF16)
    hi_ref[own, :] = mine_hi
    lo_ref[own, :] = (mine - mine_hi.astype(F32)).astype(BF16)
    pick(cut_ft, ft_ref, 1 - place_ref[1])
    g = jnp.dot(cut_ft[...], hi_ref[...], preferred_element_type=F32)
    out_ref[:half, :] = g + jnp.dot(cut_ft[...], lo_ref[...], preferred_element_type=F32)
    out_ref[half:, :] = jnp.broadcast_to(jnp.sum(value, axis=1, keepdims=True), (8, ds))


def pick(dst, src, core):
    groups = 8
    cut = dst.shape[0] // groups
    for g in range(groups):
        dst[g * cut:(g + 1) * cut, :] = src[pl.ds(pl.multiple_of((2 * g + core) * cut, cut), cut), :]


def home_kernel(place_ref, ft_ref, hi_ref, lo_ref, out_ref, cut_ft):
    pick(cut_ft, ft_ref, place_ref[1])
    out_ref[...] = jnp.dot(cut_ft[...], hi_ref[...], preferred_element_type=F32) + jnp.dot(
        cut_ft[...], lo_ref[...], preferred_element_type=F32)


def packed(loss):
    hi = loss.astype(BF16).astype(F32)
    mid = (loss - hi).astype(BF16).astype(F32)
    low = loss - hi - mid
    row = lax.broadcasted_iota(jnp.int32, loss.shape, 0)
    out = jnp.where(row == 0, hi, jnp.where(row == 1, mid, jnp.where(row == 2, low, 0.0)))
    return jnp.concatenate([out, jnp.zeros_like(out)], axis=0).astype(BF16)


def unpacked(rows):
    rows = rows.astype(F32)
    return rows[0:1, :] + rows[1:2, :] + rows[2:3, :]


def cores_kernel(xn, place_ref, home_ref, got_ref, away_ref, keep_ref, *sends):
    half = home_ref.shape[0]
    cut = half // xn
    loss = got_ref[half:, :] + away_ref[half:, :]
    x = place_ref[2]
    at = pl.ds(pl.multiple_of(x * cut, cut), cut)
    keep_ref[:cut, :] = home_ref[at, :] + got_ref[at, :]
    keep_ref[cut:, :] = loss
    rows = packed(loss)
    for k, ref in zip((1, 3, 2), sends):
        at = pl.ds(pl.multiple_of(lax.rem(x + k, xn) * cut, cut), cut)
        ref[:cut, :] = (home_ref[at, :] + got_ref[at, :]).astype(BF16)
        ref[cut:, :] = rows


def rows_kernel(place_ref, keep_ref, p_ref, q_ref, r_ref, mine_ref, across_ref, other_ref, total):
    cut = keep_ref.shape[0] - 8
    half = cut // 2
    total[...] = keep_ref[:cut, :]
    loss = keep_ref[cut:, :]
    for ref in (p_ref, q_ref, r_ref):
        total[...] += ref[:cut, :].astype(F32)
        loss = loss + unpacked(ref[cut:, :])
    y = place_ref[3]
    mine_ref[:half, :] = total[pl.ds(pl.multiple_of(y * half, half), half), :]
    mine_ref[half:, :] = loss
    across_ref[:half, :] = mine_ref[:half, :].astype(BF16)
    across_ref[half:, :] = packed(loss)
    other_ref[:half, :] = total[pl.ds(pl.multiple_of((1 - y) * half, half), half), :]
    other_ref[half:, :] = loss


def plane_kernel(mine_ref, p_ref, q_ref, r_ref, out_ref, loss_ref):
    half = out_ref.shape[0]
    out_ref[...] = mine_ref[:half, :] + p_ref[:half, :] + q_ref[:half, :] + r_ref[:half, :].astype(F32)
    loss = mine_ref[half:, :] + p_ref[half:, :] + q_ref[half:, :] + unpacked(r_ref[half:, :])
    loss_ref[...] = loss[:, :LANES]


def merge(*parts):
    top = functools.reduce(jnp.maximum, [p[0:1, :] for p in parts])
    out = [0.0] * 4
    for p in parts:
        w = jnp.exp2(p[0:1, :] - top)
        out = [out[0] + w * p[1:2, :], out[1] + p[2:3, :], out[2] + w * p[3:4, :], out[3] + p[4:5, :]]
    return jnp.concatenate([top] + out + [jnp.zeros((3, top.shape[1]), F32)], axis=0)


def near_kernel(own_ref, above_ref, below_ref, after_ref, pair_ref, window_ref):
    pair = merge(own_ref[...], above_ref[...])
    pair_ref[...] = pair
    window_ref[...] = merge(pair, below_ref[...])


def per_device(features, proj, student_text, teacher_image, teacher_text):
    rows, feat = features.shape
    dt = teacher_text.shape[1]
    ds = student_text.shape[1]
    zn, yn, xn, cn = (lax.axis_size(a) for a in ("z", Y, "x", "c"))
    images = rows * zn
    batch = images * yn * xn * cn
    texts = rows * yn * xn * cn
    column = rows * yn
    gain = float(teacher_gain / np.sqrt(np.float32(dt)))
    half = feat // cn
    place = jnp.stack([lax.axis_index(a) for a in ("z", "c", "x", "yl")]).astype(jnp.int32)

    swap = lambda v: lax.ppermute(v, "c", flip(cn, 1))
    raw = (features, student_text, teacher_image, teacher_text)
    img = jnp.concatenate([teacher_image, features], axis=1)
    txt = jnp.concatenate([teacher_text, student_text], axis=1)
    txts, imgs, st_own = pl.pallas_call(
        chip_kernel,
        in_specs=[SMEM] + [VMEM] * 6,
        out_specs=[VMEM] * 3,
        out_shape=[shape((rows, dt + ds), BF16), shape((2 * rows, dt + feat), BF16), shape((rows, ds), BF16)],
        compiler_params=params(),
        cost_estimate=FREE,
        name="chip",
    )(place, img, txt, *(swap(v) for v in raw))

    def plane(v, step, stage):
        pairs = []
        dims = (yn // 2, xn, 2, cn)
        for src in np.ndindex(*dims):
            yh, x, yl, c = src
            y = 2 * yh + yl
            if c == stage:
                y = (y + step) % yn
            else:
                x = (x + step) % xn
            dst = (y // 2, x, y % 2, c)
            pairs.append((int(np.ravel_multi_index(src, dims)), int(np.ravel_multi_index(dst, dims))))
        return lax.ppermute(v, ("yh", "x", "yl", "c"), pairs)

    def climb(v, step):
        pairs = [(z * cn + c, (z + (step if c == 0 else -step)) % zn * cn + c) for z in range(zn) for c in range(cn)]
        return lax.ppermute(v, ("z", "c"), pairs)

    together = lax.optimization_barrier
    left, right, far, one = together((plane(txts, 1, 0), plane(txts, -1, 0), plane(txts, 2, 0), climb(imgs, 1)))
    two = climb(imgs, 2)
    own_col = pl.pallas_call(
        column_kernel,
        in_specs=[VMEM] * 4,
        out_specs=VMEM,
        out_shape=shape((column, dt + ds), BF16),
        compiler_params=params(),
        name="column",
    )(txts, left, right, far)
    left_col, right_col = plane(own_col, 1, 1), plane(own_col, -1, 1)
    far_col = plane(left_col, 1, 1)
    onward, across = pl.pallas_call(
        onward_kernel,
        in_specs=[VMEM] * 2,
        out_specs=[VMEM] * 2,
        out_shape=[shape((3 * rows, dt + feat), BF16), shape((2 * rows, dt + feat), BF16)],
        compiler_params=params(),
        cost_estimate=FREE,
        name="onward",
    )(one, two)
    ahead = climb(onward, 2)
    near = swap(across)
    third = swap(ahead[rows:2 * rows])

    timg, feats, simg, simgb, inv, self_col, diag = pl.pallas_call(
        functools.partial(images_kernel, zn, dt),
        in_specs=[SMEM] + [VMEM] * 8,
        out_specs=[VMEM] * 7,
        out_shape=[shape((images, dt), BF16), shape((images, feat), BF16), shape((images, ds), F32), shape((images, ds), BF16),
                   shape((images, LANES), F32), shape((images, LANES), F32), shape((rows, ds), F32)],
        compiler_params=params(),
        cost_estimate=FREE,
        name="images",
    )(place, st_own, proj, imgs, one, two, ahead, near, third)

    blocks = [(own_col, swap(own_col)), (left_col, swap(left_col)), (right_col, swap(right_col)), None]
    span = column * cn
    stat = self_col
    chain = []
    stats = []
    for n, block in enumerate(blocks):
        final = n == len(blocks) - 1
        if final:
            block = (far_col, swap(far_col))
        big = [shape((images, texts), BF16)] * 3 + [shape((texts, ds), BF16), shape((images, 5 * LANES), F32), shape((images, LANES), F32)]
        out = pl.pallas_call(
            make_block(n, final, gain, [v.shape[0] for v in block]),
            in_specs=[VMEM] * (3 + len(block) + len(chain)),
            out_specs=[VMEM] * (7 if final else 6),
            out_shape=big + ([shape((8, images), F32)] if final else []),
            scratch_shapes=[pltpu.VMEM((images, span), F32)] * 2,
            input_output_aliases={3 + len(block) + k: k for k in range(len(chain))} | ({2: 4} if n else {}),
            compiler_params=params(),
            cost_estimate=FREE,
            name="block" + str(n),
        )(timg, simgb, stat, *block, *chain)
        chain, stat = list(out[:4]), out[4]
        stats.append(out[5])
        if n == 1:
            far_col, stat = together((far_col, stat))
    flat = out[6]
    te, se, sig, stu = chain

    a, c, ft, done_student = pl.pallas_call(
        student_kernel,
        in_specs=[VMEM] * 6,
        out_specs=[VMEM] * 4,
        out_shape=[shape((images, ds), BF16)] * 2 + [shape((feat, images), BF16), shape((8, LANES), F32)],
        compiler_params=params(),
        cost_estimate=FREE,
        name="student",
    )(se, sig, stu, simg, inv, feats)
    b = pl.pallas_call(
        teacher_kernel,
        in_specs=[VMEM] * (4 + len(stats)),
        out_specs=VMEM,
        out_shape=shape((images, ds), BF16),
        scratch_shapes=[pltpu.VMEM((images, texts), BF16)],
        compiler_params=params(),
        cost_estimate=FREE,
        name="teacher",
    )(te, stu, simg, inv, *stats)

    below = lax.ppermute(flat, "z", ring(zn, 1))
    above = lax.ppermute(flat, "z", ring(zn, zn - 1))
    pair, window = pl.pallas_call(
        near_kernel,
        in_specs=[VMEM] * 4,
        out_specs=[VMEM] * 2,
        out_shape=[shape((8, images), F32)] * 2,
        compiler_params=params(),
        name="near",
    )(flat, above, below, done_student)
    ahead = lax.ppermute(window, "z", ring(zn, zn - 3))
    behind = lax.ppermute(pair, "z", ring(zn, 3))

    away, hi, lo, val = pl.pallas_call(
        away_kernel,
        in_specs=[SMEM] + [VMEM] * 9,
        out_specs=[VMEM] * 4,
        out_shape=[shape((half + 8, ds), F32), shape((images, ds), BF16), shape((images, ds), BF16), shape((8, images), F32)],
        scratch_shapes=[pltpu.VMEM((images, LANES), F32), pltpu.VMEM((half, images), BF16)],
        compiler_params=params(),
        cost_estimate=FREE,
        name="away",
    )(place, window, ahead, behind, flat, a, b, c, diag, ft)
    arrived = swap(away)
    home = pl.pallas_call(
        home_kernel,
        in_specs=[SMEM] + [VMEM] * 3,
        out_specs=VMEM,
        out_shape=shape((half, ds), F32),
        scratch_shapes=[pltpu.VMEM((half, images), BF16)],
        compiler_params=params(),
        cost_estimate=FREE,
        name="home",
    )(place, ft, hi, lo)

    cut = half // xn
    keep, *sends = pl.pallas_call(
        functools.partial(cores_kernel, xn),
        in_specs=[SMEM] + [VMEM] * 3,
        out_specs=[VMEM] * 4,
        out_shape=[shape((cut + 8, ds), F32)] + [shape((cut + 16, ds), BF16)] * 3,
        compiler_params=params(),
        name="cores",
    )(place, home, arrived, away)
    got = [lax.ppermute(v, "x", ring(xn, k)) for k, v in zip((1, 3, 2), sends)]
    cut = cut // 2
    mine, across, other = pl.pallas_call(
        rows_kernel,
        in_specs=[SMEM] + [VMEM] * 4,
        out_specs=[VMEM] * 3,
        out_shape=[shape((cut + 8, ds), F32), shape((cut + 16, ds), BF16), shape((cut + 8, ds), F32)],
        scratch_shapes=[pltpu.VMEM((2 * cut, ds), F32)],
        compiler_params=params(),
        name="rows",
    )(place, keep, *got)
    own, loss = pl.pallas_call(
        plane_kernel,
        in_specs=[VMEM] * 4,
        out_specs=[VMEM] * 2,
        out_shape=[shape((cut, ds), F32), shape((8, LANES), F32)],
        compiler_params=params(),
        name="plane",
    )(mine, lax.ppermute(other, Y, ring(yn, 1)), lax.ppermute(other, Y, ring(yn, 3)), lax.ppermute(across, Y, ring(yn, 2)))

    below = lax.ppermute(own, "z", ring(zn, 1))
    above = lax.ppermute(own, "z", ring(zn, zn - 1))
    pair = own + above
    window = pair + below
    ahead = lax.ppermute(window.astype(BF16), "z", ring(zn, zn - 3))
    behind = lax.ppermute(pair.astype(BF16), "z", ring(zn, 3))
    grad = window + ahead.astype(F32) + behind.astype(F32)

    row_loss = lax.dynamic_slice_in_dim(val[0], lax.axis_index("z") * rows, rows, 0)
    return (row_loss, loss[0, 0] / batch, grad)


def solution(mesh):
    sizes = dict(mesh.shape)
    fine = Mesh(np.asarray(mesh.devices).reshape(sizes["blk"] // 2, 2, sizes["img"] // 4, 2, 2), ALL)
    return jax.shard_map(
        per_device,
        mesh=fine,
        in_specs=(P(ALL, None), P(), P(ALL, None), P(ALL, None), P(ALL, None)),
        out_specs=(P(ALL), P(), P(("x", "yl", "c"), None)),
        check_vma=False,
    )
```

```python
import functools

import jax
import jax.numpy as jnp
import numpy as np
from jax import lax
from jax.experimental import pallas as pl
from jax.experimental.pallas import tpu as pltpu
from jax.sharding import Mesh, PartitionSpec as P

sig_scale = 10.0
sig_bias = -10.0
teacher_gain = 3.0
eps_value = 1e-06

F32 = jnp.float32
BF16 = jnp.bfloat16
LOG2E = float(np.log2(np.e))
LN2 = float(np.log(2.0))
NT = (((1,), (1,)), ((), ()))
ALL = ("z", "yh", "x", "yl", "c")
Y = ("yh", "yl")
VMEM_LIMIT = 8 * 1024 * 1024
FREE = pl.CostEstimate(flops=1, bytes_accessed=1, transcendentals=0)
LANES = 128
STEP = 8
GROUP = 128
PART = 256


def ring(n, k):
    return [(i, (i + k) % n) for i in range(n)]


def flip(n, k):
    return [(i, i ^ k) for i in range(n)]


SMEM = pl.BlockSpec(memory_space=pltpu.SMEM)
VMEM = pl.BlockSpec(memory_space=pltpu.VMEM)


def shape(dims, dtype):
    return jax.ShapeDtypeStruct(dims, dtype)


def params():
    return pltpu.CompilerParams(vmem_limit_bytes=VMEM_LIMIT)


def chip_kernel(place_ref, img_ref, txt_ref, feat2_ref, txt2_ref, timg2_ref, ttxt2_ref, txts_ref, imgs_ref, stxt_ref):
    rows, dt = ttxt2_ref.shape
    half = rows // 2
    mine = pl.ds(pl.multiple_of(place_ref[1] * half, half), half)
    stxt_ref[...] = unit(txt_ref[:, dt:])
    txts_ref[:half, :dt] = txt_ref[mine, :dt]
    txts_ref[half:, :dt] = ttxt2_ref[mine, :]
    txts_ref[:half, dt:] = stxt_ref[mine, :]
    txts_ref[half:, dt:] = unit(txt2_ref[mine, :])
    imgs_ref[:rows, :] = img_ref[...]
    imgs_ref[rows:, :dt] = timg2_ref[...]
    imgs_ref[rows:, dt:] = feat2_ref[...]


def unit(txt):
    txt = txt.astype(F32)
    return (txt / jnp.sqrt(jnp.sum(txt * txt, axis=1, keepdims=True) + eps_value)).astype(BF16)


def onward_kernel(one_ref, two_ref, on_ref, across_ref):
    rows = one_ref.shape[0] // 2
    on_ref[:2 * rows, :] = one_ref[...]
    on_ref[2 * rows:, :] = two_ref[:rows, :]
    across_ref[:rows, :] = one_ref[rows:, :]
    across_ref[rows:, :] = two_ref[rows:, :]


def column_kernel(a_ref, b_ref, c_ref, d_ref, out_ref):
    rows = a_ref.shape[0]
    for n, ref in enumerate((a_ref, b_ref, c_ref, d_ref)):
        out_ref[n * rows:(n + 1) * rows, :] = ref[...]


def ring_rows(place_ref, zn, rows, shift):
    side = 1 - 2 * place_ref[1]
    return pl.ds(pl.multiple_of(lax.rem(place_ref[0] + side * shift + zn, zn) * rows, rows), rows)


def embed(zn, dt, place_ref, proj_ref, pieces, shifts, outs, feats):
    timg_ref, feat_ref, simg_ref, simgb_ref, inv_ref = outs
    rows = feats.shape[0] // len(pieces)
    for k, ((ref, n), shift) in enumerate(zip(pieces, shifts)):
        at = ring_rows(place_ref, zn, rows, shift)
        timg_ref[at, :] = ref[n * rows:(n + 1) * rows, :dt]
        feats[k * rows:(k + 1) * rows, :] = ref[n * rows:(n + 1) * rows, dt:]
        feat_ref[at, :] = feats[k * rows:(k + 1) * rows, :]
    pre = jnp.dot(feats[...], proj_ref[...], preferred_element_type=F32)
    norm = jnp.sqrt(jnp.sum(pre * pre, axis=1, keepdims=True) + eps_value)
    simg = pre / norm
    inv = jnp.broadcast_to(1.0 / norm, (feats.shape[0], LANES))
    for k, shift in enumerate(shifts):
        at = ring_rows(place_ref, zn, rows, shift)
        part = slice(k * rows, (k + 1) * rows)
        simg_ref[at, :] = simg[part, :]
        simgb_ref[at, :] = simg[part, :].astype(BF16)
        inv_ref[at, :] = inv[part, :]
    return rows


def early_kernel(zn, dt, place_ref, proj_ref, own_txt_ref, img_ref, one_ref, two_ref, near_ref, *refs):
    outs, (self_ref, diag_ref, done_ref, feats) = refs[:5], refs[5:]
    pieces = [(img_ref, 0), (one_ref, 0), (two_ref, 0), (near_ref, 0), (near_ref, 1)]
    rows = embed(zn, dt, place_ref, proj_ref, pieces, (0, -1, -2, 1, 2), outs, feats)
    done_ref[...] = jnp.zeros_like(done_ref)
    own = ring_rows(place_ref, zn, rows, 0)
    s = outs[2][own, :]
    txt = own_txt_ref[...].astype(F32)
    margin = sig_scale * jnp.sum(s.astype(BF16).astype(F32) * txt, axis=1, keepdims=True) + sig_bias
    self_ref[...] = jnp.zeros_like(self_ref)
    lane = lax.broadcasted_iota(jnp.int32, (rows, LANES), 1)
    self_ref[own, :] = jnp.where(lane == 0, -margin, 0.0)
    d = -sig_scale * txt
    diag_ref[...] = (d - s * jnp.sum(s * d, axis=1, keepdims=True)) * outs[4][own, 0:1]


def late_kernel(zn, dt, place_ref, proj_ref, ahead_ref, third_ref, *refs):
    embed(zn, dt, place_ref, proj_ref, [(ahead_ref, 0), (third_ref, 0), (ahead_ref, 2)], (-3, 3, zn // 2), refs[6:11], refs[11])


def make_block(index, last, gain, sizes):
    first = index == 0
    span = sum(sizes)

    def kernel(timg_ref, simgb_ref, old_ref, *refs):
        texts, refs = refs[:len(sizes)], refs[len(sizes):]
        if not first:
            refs = refs[4:]
        te_ref, se_ref, sig_ref, stu_ref, stat_ref, top_ref = refs[:6]
        flat_ref = refs[6] if last else None
        tl, sl = refs[-2:]
        dt = timg_ref.shape[1]
        images = timg_ref.shape[0]
        cols = slice(index * span, (index + 1) * span)
        shrink = float(np.exp(sig_bias))
        fold = lambda v: sum((v[:, k:k + LANES] for k in range(LANES, span, LANES)), v[:, :LANES])
        at = 0
        for ref, n in zip(texts, sizes):
            stu_ref[index * span + at:index * span + at + n, :] = ref[:, dt:]
            at += n
        at = 0
        for ref, n in zip(texts, sizes):
            tl[:, at:at + n] = lax.dot_general(timg_ref[...], ref[:, :dt], NT, preferred_element_type=F32)
            sl[:, at:at + n] = lax.dot_general(simgb_ref[...], ref[:, dt:], NT, preferred_element_type=F32)
            at += n

        def body(k, none):
            for u in range(0, GROUP, 2 * STEP):
                at = pl.multiple_of(k * GROUP + u, 2 * STEP)
                outs = []
                for half in range(2):
                    rows = pl.ds(pl.multiple_of(at + half * STEP, STEP), STEP)
                    t = (gain * LOG2E) * tl[rows, :]
                    s = (sig_scale * LOG2E) * sl[rows, :]
                    top = jnp.max(t, axis=1, keepdims=True)
                    if not first:
                        top = jnp.maximum(top, old_ref[rows, :LANES])
                    top = jnp.broadcast_to(top, (STEP, LANES))
                    te = jnp.exp2(t - jnp.concatenate([top] * (span // LANES), axis=1))
                    se = jnp.exp2(s)
                    em = se * shrink
                    up = 1.0 + em
                    sig = em * pl.reciprocal(up, approx=True)
                    soft = jnp.log(up) + (em - (up - 1.0))
                    outs.append((te, se, sig))
                    sums = [fold(te), fold(se), fold(te * (t - s)), fold(soft)]
                    if first:
                        sums[3] = sums[3] + old_ref[rows, :]
                    else:
                        w = jnp.exp2(old_ref[rows, :LANES] - top)
                        was = [old_ref[rows, j * LANES:(j + 1) * LANES] for j in range(1, 5)]
                        sums = [sums[0] + w * was[0], sums[1] + was[1], sums[2] + w * was[2], sums[3] + was[3]]
                    top_ref[rows, :] = top
                    for j, v in enumerate([top] + sums):
                        stat_ref[rows, j * LANES:(j + 1) * LANES] = v
                for ref, low, high in zip((te_ref, se_ref, sig_ref), *outs):
                    ref[pl.ds(at, 2 * STEP), cols] = jnp.concatenate([low, high], axis=0).astype(BF16)
            return none

        lax.fori_loop(0, images // GROUP, body, 0)
        if last:
            ones = jnp.ones((8, LANES), F32)
            out = [stat_ref[:, :LANES].T[:1, :]]
            for k in range(1, 5):
                v = lax.dot_general(ones, stat_ref[:, k * LANES:(k + 1) * LANES], NT, precision=lax.Precision.HIGHEST, preferred_element_type=F32)
                out.append(v[:1, :])
            flat_ref[...] = jnp.concatenate(out + [jnp.zeros((3, images), F32)], axis=0)

    return kernel


def carry(weights, txt, simg, inv):
    d = jnp.dot(weights, txt, preferred_element_type=F32)
    along = jnp.sum(simg * d, axis=1, keepdims=True)
    return ((d - simg * along) * inv).astype(BF16)


def student_kernel(se_ref, sig_ref, stu_ref, simg_ref, inv_ref, feat_ref, a_ref, c_ref, ft_ref, done_ref):
    def part(p, none):
        rows = pl.ds(pl.multiple_of(p * PART, PART), PART)
        for src, dst in ((se_ref, a_ref), (sig_ref, c_ref)):
            dst[rows, :] = carry(src[rows, :], stu_ref[...], simg_ref[rows, :], inv_ref[rows, 0:1])
        return none

    lax.fori_loop(0, se_ref.shape[0] // PART, part, 0)
    ft_ref[...] = feat_ref[...].T
    done_ref[...] = jnp.zeros_like(done_ref)


def teacher_kernel(te_ref, stu_ref, simg_ref, inv_ref, *refs):
    stats, (b_ref, scaled) = refs[:-2], refs[-2:]
    span = te_ref.shape[1] // len(stats)

    def part(p, none):
        rows = pl.ds(pl.multiple_of(p * PART, PART), PART)
        top = stats[-1][rows, 0:1]
        for n, stat in enumerate(stats):
            cols = slice(n * span, (n + 1) * span)
            w = jnp.exp2(stat[rows, 0:1] - top)
            scaled[rows, cols] = (te_ref[rows, cols].astype(F32) * w).astype(BF16)
        b_ref[rows, :] = carry(scaled[rows, :], stu_ref[...], simg_ref[rows, :], inv_ref[rows, 0:1])
        return none

    lax.fori_loop(0, te_ref.shape[0] // PART, part, 0)


def away_kernel(place_ref, window_ref, ahead_ref, behind_ref, flat_ref, a_ref, b_ref, c_ref, diag_ref, ft_ref,
                out_ref, hi_ref, lo_ref, val_ref, turned, cut_ft):
    rows = diag_ref.shape[0]
    half, ds = cut_ft.shape[0], a_ref.shape[1]
    sums = merge(window_ref[...], ahead_ref[...], behind_ref[...])
    top, tsum, ssum, tval, soft = (sums[k:k + 1, :] for k in range(5))
    value = tval / tsum * LN2 + soft - (top * LN2 + jnp.log(tsum)) + jnp.log(ssum)
    val_ref[...] = jnp.broadcast_to(value, val_ref.shape)
    ca = sig_scale / ssum
    cb = -sig_scale * jnp.exp2(flat_ref[0:1, :] - top) / tsum
    row = lax.broadcasted_iota(jnp.int32, (LANES, ca.shape[1]), 0)
    turned[...] = jnp.where(row == 0, ca, cb).T

    def part(p, none):
        some = pl.ds(pl.multiple_of(p * LANES, LANES), LANES)
        d = turned[some, 0:1] * a_ref[some, :].astype(F32) + turned[some, 1:2] * b_ref[some, :].astype(F32)
        d = d + sig_scale * c_ref[some, :].astype(F32)
        hi = d.astype(BF16)
        hi_ref[some, :] = hi
        lo_ref[some, :] = (d - hi.astype(F32)).astype(BF16)
        return none

    lax.fori_loop(0, hi_ref.shape[0] // LANES, part, 0)
    own = pl.ds(pl.multiple_of(place_ref[0] * rows, rows), rows)
    mine = hi_ref[own, :].astype(F32) + lo_ref[own, :].astype(F32) + diag_ref[...]
    mine_hi = mine.astype(BF16)
    hi_ref[own, :] = mine_hi
    lo_ref[own, :] = (mine - mine_hi.astype(F32)).astype(BF16)
    pick(cut_ft, ft_ref, 1 - place_ref[1])
    g = jnp.dot(cut_ft[...], hi_ref[...], preferred_element_type=F32)
    out_ref[:half, :] = g + jnp.dot(cut_ft[...], lo_ref[...], preferred_element_type=F32)
    out_ref[half:, :] = jnp.broadcast_to(jnp.sum(value, axis=1, keepdims=True), (8, ds))


def pick(dst, src, core):
    groups = 8
    cut = dst.shape[0] // groups
    for g in range(groups):
        dst[g * cut:(g + 1) * cut, :] = src[pl.ds(pl.multiple_of((2 * g + core) * cut, cut), cut), :]


def home_kernel(place_ref, ft_ref, hi_ref, lo_ref, out_ref, cut_ft):
    pick(cut_ft, ft_ref, place_ref[1])
    out_ref[...] = jnp.dot(cut_ft[...], hi_ref[...], preferred_element_type=F32) + jnp.dot(
        cut_ft[...], lo_ref[...], preferred_element_type=F32)


def packed(loss):
    hi = loss.astype(BF16).astype(F32)
    mid = (loss - hi).astype(BF16).astype(F32)
    low = loss - hi - mid
    row = lax.broadcasted_iota(jnp.int32, loss.shape, 0)
    out = jnp.where(row == 0, hi, jnp.where(row == 1, mid, jnp.where(row == 2, low, 0.0)))
    return jnp.concatenate([out, jnp.zeros_like(out)], axis=0).astype(BF16)


def unpacked(rows):
    rows = rows.astype(F32)
    return rows[0:1, :] + rows[1:2, :] + rows[2:3, :]


def cores_kernel(xn, place_ref, home_ref, got_ref, away_ref, keep_ref, *sends):
    half = home_ref.shape[0]
    cut = half // xn
    loss = got_ref[half:, :] + away_ref[half:, :]
    x = place_ref[2]
    at = pl.ds(pl.multiple_of(x * cut, cut), cut)
    keep_ref[:cut, :] = home_ref[at, :] + got_ref[at, :]
    keep_ref[cut:, :] = loss
    rows = packed(loss)
    for k, ref in zip((1, 3, 2), sends):
        at = pl.ds(pl.multiple_of(lax.rem(x + k, xn) * cut, cut), cut)
        ref[:cut, :] = (home_ref[at, :] + got_ref[at, :]).astype(BF16)
        ref[cut:, :] = rows


def rows_kernel(place_ref, keep_ref, p_ref, q_ref, r_ref, mine_ref, across_ref, other_ref, total):
    cut = keep_ref.shape[0] - 8
    half = cut // 2
    total[...] = keep_ref[:cut, :]
    loss = keep_ref[cut:, :]
    for ref in (p_ref, q_ref, r_ref):
        total[...] += ref[:cut, :].astype(F32)
        loss = loss + unpacked(ref[cut:, :])
    y = place_ref[3]
    mine_ref[:half, :] = total[pl.ds(pl.multiple_of(y * half, half), half), :]
    mine_ref[half:, :] = loss
    across_ref[:half, :] = mine_ref[:half, :].astype(BF16)
    across_ref[half:, :] = packed(loss)
    other_ref[:half, :] = total[pl.ds(pl.multiple_of((1 - y) * half, half), half), :]
    other_ref[half:, :] = loss


def plane_kernel(mine_ref, p_ref, q_ref, r_ref, out_ref, loss_ref):
    half = out_ref.shape[0]
    out_ref[...] = mine_ref[:half, :] + p_ref[:half, :] + q_ref[:half, :] + r_ref[:half, :].astype(F32)
    loss = mine_ref[half:, :] + p_ref[half:, :] + q_ref[half:, :] + unpacked(r_ref[half:, :])
    loss_ref[...] = loss[:, :LANES]


def merge(*parts):
    top = functools.reduce(jnp.maximum, [p[0:1, :] for p in parts])
    out = [0.0] * 4
    for p in parts:
        w = jnp.exp2(p[0:1, :] - top)
        out = [out[0] + w * p[1:2, :], out[1] + p[2:3, :], out[2] + w * p[3:4, :], out[3] + p[4:5, :]]
    return jnp.concatenate([top] + out + [jnp.zeros((3, top.shape[1]), F32)], axis=0)


def near_kernel(own_ref, above_ref, below_ref, after_ref, pair_ref, window_ref):
    pair = merge(own_ref[...], above_ref[...])
    pair_ref[...] = pair
    window_ref[...] = merge(pair, below_ref[...])


def per_device(features, proj, student_text, teacher_image, teacher_text):
    rows, feat = features.shape
    dt = teacher_text.shape[1]
    ds = student_text.shape[1]
    zn, yn, xn, cn = (lax.axis_size(a) for a in ("z", Y, "x", "c"))
    images = rows * zn
    batch = images * yn * xn * cn
    texts = rows * yn * xn * cn
    column = rows * yn
    gain = float(teacher_gain / np.sqrt(np.float32(dt)))
    half = feat // cn
    place = jnp.stack([lax.axis_index(a) for a in ("z", "c", "x", "yl")]).astype(jnp.int32)

    swap = lambda v: lax.ppermute(v, "c", flip(cn, 1))
    raw = (features, student_text, teacher_image, teacher_text)
    img = jnp.concatenate([teacher_image, features], axis=1)
    txt = jnp.concatenate([teacher_text, student_text], axis=1)
    txts, imgs, st_own = pl.pallas_call(
        chip_kernel,
        in_specs=[SMEM] + [VMEM] * 6,
        out_specs=[VMEM] * 3,
        out_shape=[shape((rows, dt + ds), BF16), shape((2 * rows, dt + feat), BF16), shape((rows, ds), BF16)],
        compiler_params=params(),
        cost_estimate=FREE,
        name="chip",
    )(place, img, txt, *(swap(v) for v in raw))

    def plane(v, step, stage):
        pairs = []
        dims = (yn // 2, xn, 2, cn)
        for src in np.ndindex(*dims):
            yh, x, yl, c = src
            y = 2 * yh + yl
            if c == stage:
                y = (y + step) % yn
            else:
                x = (x + step) % xn
            dst = (y // 2, x, y % 2, c)
            pairs.append((int(np.ravel_multi_index(src, dims)), int(np.ravel_multi_index(dst, dims))))
        return lax.ppermute(v, ("yh", "x", "yl", "c"), pairs)

    def climb(v, step):
        pairs = [(z * cn + c, (z + (step if c == 0 else -step)) % zn * cn + c) for z in range(zn) for c in range(cn)]
        return lax.ppermute(v, ("z", "c"), pairs)

    together = lax.optimization_barrier
    left, right, far, one = together((plane(txts, 1, 0), plane(txts, -1, 0), plane(txts, 2, 0), climb(imgs, 1)))
    two = climb(imgs, 2)
    own_col = pl.pallas_call(
        column_kernel,
        in_specs=[VMEM] * 4,
        out_specs=VMEM,
        out_shape=shape((column, dt + ds), BF16),
        compiler_params=params(),
        name="column",
    )(txts, left, right, far)
    left_col, right_col = plane(own_col, 1, 1), plane(own_col, -1, 1)
    onward, across = pl.pallas_call(
        onward_kernel,
        in_specs=[VMEM] * 2,
        out_specs=[VMEM] * 2,
        out_shape=[shape((3 * rows, dt + feat), BF16), shape((2 * rows, dt + feat), BF16)],
        compiler_params=params(),
        cost_estimate=FREE,
        name="onward",
    )(one, two)
    ahead = climb(onward, 2)
    near = swap(across)
    arrays = [shape((images, dt), BF16), shape((images, feat), BF16), shape((images, ds), F32), shape((images, ds), BF16), shape((images, LANES), F32)]
    *arrays_early, self_col, diag, done_early = pl.pallas_call(
        functools.partial(early_kernel, zn, dt),
        in_specs=[SMEM] + [VMEM] * 6,
        out_specs=[VMEM] * 8,
        out_shape=arrays + [shape((images, LANES), F32), shape((rows, ds), F32), shape((8, LANES), F32)],
        scratch_shapes=[pltpu.VMEM((5 * rows, feat), BF16)],
        compiler_params=params(),
        cost_estimate=FREE,
        name="early",
    )(place, proj, st_own, imgs, one, two, near)
    left_col, done_early = together((left_col, done_early))
    far_col = plane(left_col, 1, 1)
    third = swap(ahead[rows:2 * rows])
    timg, feats, simg, simgb, inv = pl.pallas_call(
        functools.partial(late_kernel, zn, dt),
        in_specs=[SMEM] + [VMEM] * 9,
        out_specs=[VMEM] * 5,
        out_shape=arrays,
        scratch_shapes=[pltpu.VMEM((3 * rows, feat), BF16)],
        input_output_aliases={4 + k: k for k in range(5)},
        compiler_params=params(),
        cost_estimate=FREE,
        name="late",
    )(place, proj, ahead, third, *arrays_early, done_early)

    blocks = [(own_col, swap(own_col)), (left_col, swap(left_col)), (right_col, swap(right_col)), None]
    span = column * cn
    stat = self_col
    chain = []
    stats = []
    for n, block in enumerate(blocks):
        final = n == len(blocks) - 1
        if final:
            block = (far_col, swap(far_col))
        big = [shape((images, texts), BF16)] * 3 + [shape((texts, ds), BF16), shape((images, 5 * LANES), F32), shape((images, LANES), F32)]
        out = pl.pallas_call(
            make_block(n, final, gain, [v.shape[0] for v in block]),
            in_specs=[VMEM] * (3 + len(block) + len(chain)),
            out_specs=[VMEM] * (7 if final else 6),
            out_shape=big + ([shape((8, images), F32)] if final else []),
            scratch_shapes=[pltpu.VMEM((images, span), F32)] * 2,
            input_output_aliases={3 + len(block) + k: k for k in range(len(chain))} | ({2: 4} if n else {}),
            compiler_params=params(),
            cost_estimate=FREE,
            name="block" + str(n),
        )(timg, simgb, stat, *block, *chain)
        chain, stat = list(out[:4]), out[4]
        stats.append(out[5])
        if n == 1:
            far_col, stat = together((far_col, stat))
    flat = out[6]
    te, se, sig, stu = chain

    a, c, ft, done_student = pl.pallas_call(
        student_kernel,
        in_specs=[VMEM] * 6,
        out_specs=[VMEM] * 4,
        out_shape=[shape((images, ds), BF16)] * 2 + [shape((feat, images), BF16), shape((8, LANES), F32)],
        compiler_params=params(),
        cost_estimate=FREE,
        name="student",
    )(se, sig, stu, simg, inv, feats)
    b = pl.pallas_call(
        teacher_kernel,
        in_specs=[VMEM] * (4 + len(stats)),
        out_specs=VMEM,
        out_shape=shape((images, ds), BF16),
        scratch_shapes=[pltpu.VMEM((images, texts), BF16)],
        compiler_params=params(),
        cost_estimate=FREE,
        name="teacher",
    )(te, stu, simg, inv, *stats)

    below = lax.ppermute(flat, "z", ring(zn, 1))
    above = lax.ppermute(flat, "z", ring(zn, zn - 1))
    pair, window = pl.pallas_call(
        near_kernel,
        in_specs=[VMEM] * 4,
        out_specs=[VMEM] * 2,
        out_shape=[shape((8, images), F32)] * 2,
        compiler_params=params(),
        name="near",
    )(flat, above, below, done_student)
    ahead = lax.ppermute(window, "z", ring(zn, zn - 3))
    behind = lax.ppermute(pair, "z", ring(zn, 3))

    away, hi, lo, val = pl.pallas_call(
        away_kernel,
        in_specs=[SMEM] + [VMEM] * 9,
        out_specs=[VMEM] * 4,
        out_shape=[shape((half + 8, ds), F32), shape((images, ds), BF16), shape((images, ds), BF16), shape((8, images), F32)],
        scratch_shapes=[pltpu.VMEM((images, LANES), F32), pltpu.VMEM((half, images), BF16)],
        compiler_params=params(),
        cost_estimate=FREE,
        name="away",
    )(place, window, ahead, behind, flat, a, b, c, diag, ft)
    arrived = swap(away)
    home = pl.pallas_call(
        home_kernel,
        in_specs=[SMEM] + [VMEM] * 3,
        out_specs=VMEM,
        out_shape=shape((half, ds), F32),
        scratch_shapes=[pltpu.VMEM((half, images), BF16)],
        compiler_params=params(),
        cost_estimate=FREE,
        name="home",
    )(place, ft, hi, lo)

    cut = half // xn
    keep, *sends = pl.pallas_call(
        functools.partial(cores_kernel, xn),
        in_specs=[SMEM] + [VMEM] * 3,
        out_specs=[VMEM] * 4,
        out_shape=[shape((cut + 8, ds), F32)] + [shape((cut + 16, ds), BF16)] * 3,
        compiler_params=params(),
        name="cores",
    )(place, home, arrived, away)
    got = [lax.ppermute(v, "x", ring(xn, k)) for k, v in zip((1, 3, 2), sends)]
    cut = cut // 2
    mine, across, other = pl.pallas_call(
        rows_kernel,
        in_specs=[SMEM] + [VMEM] * 4,
        out_specs=[VMEM] * 3,
        out_shape=[shape((cut + 8, ds), F32), shape((cut + 16, ds), BF16), shape((cut + 8, ds), F32)],
        scratch_shapes=[pltpu.VMEM((2 * cut, ds), F32)],
        compiler_params=params(),
        name="rows",
    )(place, keep, *got)
    own, loss = pl.pallas_call(
        plane_kernel,
        in_specs=[VMEM] * 4,
        out_specs=[VMEM] * 2,
        out_shape=[shape((cut, ds), F32), shape((8, LANES), F32)],
        compiler_params=params(),
        name="plane",
    )(mine, lax.ppermute(other, Y, ring(yn, 1)), lax.ppermute(other, Y, ring(yn, 3)), lax.ppermute(across, Y, ring(yn, 2)))

    below = lax.ppermute(own, "z", ring(zn, 1))
    above = lax.ppermute(own, "z", ring(zn, zn - 1))
    pair = own + above
    window = pair + below
    ahead = lax.ppermute(window.astype(BF16), "z", ring(zn, zn - 3))
    behind = lax.ppermute(pair.astype(BF16), "z", ring(zn, 3))
    grad = window + ahead.astype(F32) + behind.astype(F32)

    row_loss = lax.dynamic_slice_in_dim(val[0], lax.axis_index("z") * rows, rows, 0)
    return (row_loss, loss[0, 0] / batch, grad)


def solution(mesh):
    sizes = dict(mesh.shape)
    fine = Mesh(np.asarray(mesh.devices).reshape(sizes["blk"] // 2, 2, sizes["img"] // 4, 2, 2), ALL)
    return jax.shard_map(
        per_device,
        mesh=fine,
        in_specs=(P(ALL, None), P(), P(ALL, None), P(ALL, None), P(ALL, None)),
        out_specs=(P(ALL), P(), P(("x", "yl", "c"), None)),
        check_vma=False,
    )
```

```python
import functools

import jax
import jax.numpy as jnp
import numpy as np
from jax import lax
from jax.experimental import pallas as pl
from jax.experimental.pallas import tpu as pltpu
from jax.sharding import Mesh, PartitionSpec as P

sig_scale = 10.0
sig_bias = -10.0
teacher_gain = 3.0
eps_value = 1e-06

F32 = jnp.float32
BF16 = jnp.bfloat16
LOG2E = float(np.log2(np.e))
LN2 = float(np.log(2.0))
NT = (((1,), (1,)), ((), ()))
ALL = ("z", "yh", "x", "yl", "c")
Y = ("yh", "yl")
VMEM_LIMIT = 8 * 1024 * 1024
FREE = pl.CostEstimate(flops=1, bytes_accessed=1, transcendentals=0)
LANES = 128
STEP = 8
GROUP = 128
PART = 256


def ring(n, k):
    return [(i, (i + k) % n) for i in range(n)]


def flip(n, k):
    return [(i, i ^ k) for i in range(n)]


SMEM = pl.BlockSpec(memory_space=pltpu.SMEM)
VMEM = pl.BlockSpec(memory_space=pltpu.VMEM)


def shape(dims, dtype):
    return jax.ShapeDtypeStruct(dims, dtype)


def params():
    return pltpu.CompilerParams(vmem_limit_bytes=VMEM_LIMIT)


def chip_kernel(place_ref, img_ref, txt_ref, feat2_ref, txt2_ref, timg2_ref, ttxt2_ref, txts_ref, imgs_ref, stxt_ref):
    rows, dt = ttxt2_ref.shape
    half = rows // 2
    mine = pl.ds(pl.multiple_of(place_ref[1] * half, half), half)
    stxt_ref[...] = unit(txt_ref[:, dt:])
    txts_ref[:half, :dt] = txt_ref[mine, :dt]
    txts_ref[half:, :dt] = ttxt2_ref[mine, :]
    txts_ref[:half, dt:] = stxt_ref[mine, :]
    txts_ref[half:, dt:] = unit(txt2_ref[mine, :])
    imgs_ref[:rows, :] = img_ref[...]
    imgs_ref[rows:, :dt] = timg2_ref[...]
    imgs_ref[rows:, dt:] = feat2_ref[...]


def unit(txt):
    txt = txt.astype(F32)
    return (txt / jnp.sqrt(jnp.sum(txt * txt, axis=1, keepdims=True) + eps_value)).astype(BF16)


def onward_kernel(one_ref, two_ref, on_ref, across_ref):
    rows = one_ref.shape[0] // 2
    on_ref[:2 * rows, :] = one_ref[...]
    on_ref[2 * rows:, :] = two_ref[:rows, :]
    across_ref[:rows, :] = one_ref[rows:, :]
    across_ref[rows:, :] = two_ref[rows:, :]


def column_kernel(a_ref, b_ref, c_ref, d_ref, out_ref):
    rows = a_ref.shape[0]
    for n, ref in enumerate((a_ref, b_ref, c_ref, d_ref)):
        out_ref[n * rows:(n + 1) * rows, :] = ref[...]


def ring_rows(place_ref, zn, rows, shift):
    side = 1 - 2 * place_ref[1]
    return pl.ds(pl.multiple_of(lax.rem(place_ref[0] + side * shift + zn, zn) * rows, rows), rows)


def embed(zn, dt, place_ref, proj_ref, pieces, shifts, outs, feats):
    timg_ref, feat_ref, simg_ref, simgb_ref, inv_ref = outs
    rows = feats.shape[0] // len(pieces)
    for k, ((ref, n), shift) in enumerate(zip(pieces, shifts)):
        at = ring_rows(place_ref, zn, rows, shift)
        timg_ref[at, :] = ref[n * rows:(n + 1) * rows, :dt]
        feats[k * rows:(k + 1) * rows, :] = ref[n * rows:(n + 1) * rows, dt:]
        feat_ref[at, :] = feats[k * rows:(k + 1) * rows, :]
    pre = jnp.dot(feats[...], proj_ref[...], preferred_element_type=F32)
    norm = jnp.sqrt(jnp.sum(pre * pre, axis=1, keepdims=True) + eps_value)
    simg = pre / norm
    inv = jnp.broadcast_to(1.0 / norm, (feats.shape[0], LANES))
    for k, shift in enumerate(shifts):
        at = ring_rows(place_ref, zn, rows, shift)
        part = slice(k * rows, (k + 1) * rows)
        simg_ref[at, :] = simg[part, :]
        simgb_ref[at, :] = simg[part, :].astype(BF16)
        inv_ref[at, :] = inv[part, :]
    return rows


def early_kernel(zn, dt, place_ref, proj_ref, own_txt_ref, img_ref, one_ref, two_ref, near_ref, *refs):
    outs, (self_ref, diag_ref, done_ref, feats) = refs[:5], refs[5:]
    pieces = [(img_ref, 0), (one_ref, 0), (two_ref, 0), (near_ref, 0), (near_ref, 1)]
    rows = embed(zn, dt, place_ref, proj_ref, pieces, (0, -1, -2, 1, 2), outs, feats)
    done_ref[...] = jnp.zeros_like(done_ref)
    own = ring_rows(place_ref, zn, rows, 0)
    s = outs[2][own, :]
    txt = own_txt_ref[...].astype(F32)
    margin = sig_scale * jnp.sum(s.astype(BF16).astype(F32) * txt, axis=1, keepdims=True) + sig_bias
    self_ref[...] = jnp.zeros_like(self_ref)
    lane = lax.broadcasted_iota(jnp.int32, (rows, LANES), 1)
    self_ref[own, :] = jnp.where(lane == 0, -margin, 0.0)
    d = -sig_scale * txt
    diag_ref[...] = (d - s * jnp.sum(s * d, axis=1, keepdims=True)) * outs[4][own, 0:1]


def late_kernel(zn, dt, place_ref, proj_ref, ahead_ref, third_ref, *refs):
    embed(zn, dt, place_ref, proj_ref, [(ahead_ref, 0), (third_ref, 0), (ahead_ref, 2)], (-3, 3, zn // 2), refs[6:11], refs[11])


def make_block(index, last, gain, sizes):
    first = index == 0
    span = sum(sizes)

    def kernel(timg_ref, simgb_ref, old_ref, *refs):
        texts, refs = refs[:len(sizes)], refs[len(sizes):]
        if not first:
            refs = refs[4:]
        te_ref, se_ref, sig_ref, stu_ref, stat_ref, top_ref = refs[:6]
        flat_ref = refs[6] if last else None
        tl, sl = refs[-2:]
        dt = timg_ref.shape[1]
        images = timg_ref.shape[0]
        cols = slice(index * span, (index + 1) * span)
        shrink = float(np.exp(sig_bias))
        fold = lambda v: sum((v[:, k:k + LANES] for k in range(LANES, span, LANES)), v[:, :LANES])
        at = 0
        for ref, n in zip(texts, sizes):
            stu_ref[index * span + at:index * span + at + n, :] = ref[:, dt:]
            at += n
        at = 0
        for ref, n in zip(texts, sizes):
            tl[:, at:at + n] = lax.dot_general(timg_ref[...], ref[:, :dt], NT, preferred_element_type=F32)
            sl[:, at:at + n] = lax.dot_general(simgb_ref[...], ref[:, dt:], NT, preferred_element_type=F32)
            at += n

        def body(k, none):
            for u in range(0, GROUP, 2 * STEP):
                at = pl.multiple_of(k * GROUP + u, 2 * STEP)
                outs = []
                for half in range(2):
                    rows = pl.ds(pl.multiple_of(at + half * STEP, STEP), STEP)
                    t = (gain * LOG2E) * tl[rows, :]
                    s = (sig_scale * LOG2E) * sl[rows, :]
                    top = jnp.max(t, axis=1, keepdims=True)
                    if not first:
                        top = jnp.maximum(top, old_ref[rows, :LANES])
                    top = jnp.broadcast_to(top, (STEP, LANES))
                    te = jnp.exp2(t - jnp.concatenate([top] * (span // LANES), axis=1))
                    se = jnp.exp2(s)
                    em = se * shrink
                    up = 1.0 + em
                    sig = em * pl.reciprocal(up, approx=True)
                    soft = jnp.log(up) + (em - (up - 1.0))
                    outs.append((te, se, sig))
                    sums = [fold(te), fold(se), fold(te * (t - s)), fold(soft)]
                    if first:
                        sums[3] = sums[3] + old_ref[rows, :]
                    else:
                        w = jnp.exp2(old_ref[rows, :LANES] - top)
                        was = [old_ref[rows, j * LANES:(j + 1) * LANES] for j in range(1, 5)]
                        sums = [sums[0] + w * was[0], sums[1] + was[1], sums[2] + w * was[2], sums[3] + was[3]]
                    top_ref[rows, :] = top
                    for j, v in enumerate([top] + sums):
                        stat_ref[rows, j * LANES:(j + 1) * LANES] = v
                for ref, low, high in zip((te_ref, se_ref, sig_ref), *outs):
                    ref[pl.ds(at, 2 * STEP), cols] = jnp.concatenate([low, high], axis=0).astype(BF16)
            return none

        lax.fori_loop(0, images // GROUP, body, 0)
        if last:
            out = [stat_ref[:, :LANES].T[:1, :]]
            for k in range(1, 5):
                out.append(jnp.sum(stat_ref[:, k * LANES:(k + 1) * LANES].T, axis=0, keepdims=True))
            flat_ref[...] = jnp.concatenate(out + [jnp.zeros((3, images), F32)], axis=0)

    return kernel


def carry(weights, txt, simg, inv):
    d = jnp.dot(weights, txt, preferred_element_type=F32)
    along = jnp.sum(simg * d, axis=1, keepdims=True)
    return ((d - simg * along) * inv).astype(BF16)


def student_kernel(se_ref, sig_ref, stu_ref, simg_ref, inv_ref, feat_ref, a_ref, c_ref, ft_ref, done_ref):
    def part(p, none):
        rows = pl.ds(pl.multiple_of(p * PART, PART), PART)
        for src, dst in ((se_ref, a_ref), (sig_ref, c_ref)):
            dst[rows, :] = carry(src[rows, :], stu_ref[...], simg_ref[rows, :], inv_ref[rows, 0:1])
        return none

    lax.fori_loop(0, se_ref.shape[0] // PART, part, 0)
    ft_ref[...] = feat_ref[...].T
    done_ref[...] = jnp.zeros_like(done_ref)


def teacher_kernel(te_ref, stu_ref, simg_ref, inv_ref, *refs):
    stats, (b_ref, scaled) = refs[:-2], refs[-2:]
    span = te_ref.shape[1] // len(stats)

    def part(p, none):
        rows = pl.ds(pl.multiple_of(p * PART, PART), PART)
        top = stats[-1][rows, 0:1]
        for n, stat in enumerate(stats):
            cols = slice(n * span, (n + 1) * span)
            w = jnp.exp2(stat[rows, 0:1] - top)
            scaled[rows, cols] = (te_ref[rows, cols].astype(F32) * w).astype(BF16)
        b_ref[rows, :] = carry(scaled[rows, :], stu_ref[...], simg_ref[rows, :], inv_ref[rows, 0:1])
        return none

    lax.fori_loop(0, te_ref.shape[0] // PART, part, 0)


def away_kernel(place_ref, window_ref, ahead_ref, behind_ref, flat_ref, a_ref, b_ref, c_ref, diag_ref, ft_ref,
                out_ref, hi_ref, lo_ref, val_ref, turned, cut_ft):
    rows = diag_ref.shape[0]
    half, ds = cut_ft.shape[0], a_ref.shape[1]
    sums = merge(window_ref[...], ahead_ref[...], behind_ref[...])
    top, tsum, ssum, tval, soft = (sums[k:k + 1, :] for k in range(5))
    value = tval / tsum * LN2 + soft - (top * LN2 + jnp.log(tsum)) + jnp.log(ssum)
    val_ref[...] = jnp.broadcast_to(value, val_ref.shape)
    ca = sig_scale / ssum
    cb = -sig_scale * jnp.exp2(flat_ref[0:1, :] - top) / tsum
    row = lax.broadcasted_iota(jnp.int32, (LANES, ca.shape[1]), 0)
    turned[...] = jnp.where(row == 0, ca, cb).T

    def part(p, none):
        some = pl.ds(pl.multiple_of(p * LANES, LANES), LANES)
        d = turned[some, 0:1] * a_ref[some, :].astype(F32) + turned[some, 1:2] * b_ref[some, :].astype(F32)
        d = d + sig_scale * c_ref[some, :].astype(F32)
        hi = d.astype(BF16)
        hi_ref[some, :] = hi
        lo_ref[some, :] = (d - hi.astype(F32)).astype(BF16)
        return none

    lax.fori_loop(0, hi_ref.shape[0] // LANES, part, 0)
    own = pl.ds(pl.multiple_of(place_ref[0] * rows, rows), rows)
    mine = hi_ref[own, :].astype(F32) + lo_ref[own, :].astype(F32) + diag_ref[...]
    mine_hi = mine.astype(BF16)
    hi_ref[own, :] = mine_hi
    lo_ref[own, :] = (mine - mine_hi.astype(F32)).astype(BF16)
    pick(cut_ft, ft_ref, 1 - place_ref[1])
    g = jnp.dot(cut_ft[...], hi_ref[...], preferred_element_type=F32)
    out_ref[:half, :] = g + jnp.dot(cut_ft[...], lo_ref[...], preferred_element_type=F32)
    out_ref[half:, :] = jnp.broadcast_to(jnp.sum(value, axis=1, keepdims=True), (8, ds))


def pick(dst, src, core):
    groups = 8
    cut = dst.shape[0] // groups
    for g in range(groups):
        dst[g * cut:(g + 1) * cut, :] = src[pl.ds(pl.multiple_of((2 * g + core) * cut, cut), cut), :]


def home_kernel(place_ref, ft_ref, hi_ref, lo_ref, out_ref, cut_ft):
    pick(cut_ft, ft_ref, place_ref[1])
    out_ref[...] = jnp.dot(cut_ft[...], hi_ref[...], preferred_element_type=F32) + jnp.dot(
        cut_ft[...], lo_ref[...], preferred_element_type=F32)


def packed(loss):
    hi = loss.astype(BF16).astype(F32)
    mid = (loss - hi).astype(BF16).astype(F32)
    low = loss - hi - mid
    row = lax.broadcasted_iota(jnp.int32, loss.shape, 0)
    out = jnp.where(row == 0, hi, jnp.where(row == 1, mid, jnp.where(row == 2, low, 0.0)))
    return jnp.concatenate([out, jnp.zeros_like(out)], axis=0).astype(BF16)


def unpacked(rows):
    rows = rows.astype(F32)
    return rows[0:1, :] + rows[1:2, :] + rows[2:3, :]


def cores_kernel(xn, place_ref, home_ref, got_ref, away_ref, keep_ref, *sends):
    half = home_ref.shape[0]
    cut = half // xn
    loss = got_ref[half:, :] + away_ref[half:, :]
    x = place_ref[2]
    at = pl.ds(pl.multiple_of(x * cut, cut), cut)
    keep_ref[:cut, :] = home_ref[at, :] + got_ref[at, :]
    keep_ref[cut:, :] = loss
    rows = packed(loss)
    for k, ref in zip((1, 3, 2), sends):
        at = pl.ds(pl.multiple_of(lax.rem(x + k, xn) * cut, cut), cut)
        ref[:cut, :] = (home_ref[at, :] + got_ref[at, :]).astype(BF16)
        ref[cut:, :] = rows


def rows_kernel(place_ref, keep_ref, p_ref, q_ref, r_ref, mine_ref, across_ref, other_ref, total):
    cut = keep_ref.shape[0] - 8
    half = cut // 2
    total[...] = keep_ref[:cut, :]
    loss = keep_ref[cut:, :]
    for ref in (p_ref, q_ref, r_ref):
        total[...] += ref[:cut, :].astype(F32)
        loss = loss + unpacked(ref[cut:, :])
    y = place_ref[3]
    mine_ref[:half, :] = total[pl.ds(pl.multiple_of(y * half, half), half), :]
    mine_ref[half:, :] = loss
    across_ref[:half, :] = mine_ref[:half, :].astype(BF16)
    across_ref[half:, :] = packed(loss)
    other_ref[:half, :] = total[pl.ds(pl.multiple_of((1 - y) * half, half), half), :]
    other_ref[half:, :] = loss


def plane_kernel(mine_ref, p_ref, q_ref, r_ref, out_ref, loss_ref):
    half = out_ref.shape[0]
    out_ref[...] = mine_ref[:half, :] + p_ref[:half, :] + q_ref[:half, :] + r_ref[:half, :].astype(F32)
    loss = mine_ref[half:, :] + p_ref[half:, :] + q_ref[half:, :] + unpacked(r_ref[half:, :])
    loss_ref[...] = loss[:, :LANES]


def merge(*parts):
    top = functools.reduce(jnp.maximum, [p[0:1, :] for p in parts])
    out = [0.0] * 4
    for p in parts:
        w = jnp.exp2(p[0:1, :] - top)
        out = [out[0] + w * p[1:2, :], out[1] + p[2:3, :], out[2] + w * p[3:4, :], out[3] + p[4:5, :]]
    return jnp.concatenate([top] + out + [jnp.zeros((3, top.shape[1]), F32)], axis=0)


def near_kernel(own_ref, above_ref, below_ref, after_ref, pair_ref, window_ref):
    pair = merge(own_ref[...], above_ref[...])
    pair_ref[...] = pair
    window_ref[...] = merge(pair, below_ref[...])


def per_device(features, proj, student_text, teacher_image, teacher_text):
    rows, feat = features.shape
    dt = teacher_text.shape[1]
    ds = student_text.shape[1]
    zn, yn, xn, cn = (lax.axis_size(a) for a in ("z", Y, "x", "c"))
    images = rows * zn
    batch = images * yn * xn * cn
    texts = rows * yn * xn * cn
    column = rows * yn
    gain = float(teacher_gain / np.sqrt(np.float32(dt)))
    half = feat // cn
    place = jnp.stack([lax.axis_index(a) for a in ("z", "c", "x", "yl")]).astype(jnp.int32)

    swap = lambda v: lax.ppermute(v, "c", flip(cn, 1))
    raw = (features, student_text, teacher_image, teacher_text)
    img = jnp.concatenate([teacher_image, features], axis=1)
    txt = jnp.concatenate([teacher_text, student_text], axis=1)
    txts, imgs, st_own = pl.pallas_call(
        chip_kernel,
        in_specs=[SMEM] + [VMEM] * 6,
        out_specs=[VMEM] * 3,
        out_shape=[shape((rows, dt + ds), BF16), shape((2 * rows, dt + feat), BF16), shape((rows, ds), BF16)],
        compiler_params=params(),
        cost_estimate=FREE,
        name="chip",
    )(place, img, txt, *(swap(v) for v in raw))

    def plane(v, step, stage):
        pairs = []
        dims = (yn // 2, xn, 2, cn)
        for src in np.ndindex(*dims):
            yh, x, yl, c = src
            y = 2 * yh + yl
            if c == stage:
                y = (y + step) % yn
            else:
                x = (x + step) % xn
            dst = (y // 2, x, y % 2, c)
            pairs.append((int(np.ravel_multi_index(src, dims)), int(np.ravel_multi_index(dst, dims))))
        return lax.ppermute(v, ("yh", "x", "yl", "c"), pairs)

    def climb(v, step):
        pairs = [(z * cn + c, (z + (step if c == 0 else -step)) % zn * cn + c) for z in range(zn) for c in range(cn)]
        return lax.ppermute(v, ("z", "c"), pairs)

    together = lax.optimization_barrier
    left, right, far, one = together((plane(txts, 1, 0), plane(txts, -1, 0), plane(txts, 2, 0), climb(imgs, 1)))
    two = climb(imgs, 2)
    own_col = pl.pallas_call(
        column_kernel,
        in_specs=[VMEM] * 4,
        out_specs=VMEM,
        out_shape=shape((column, dt + ds), BF16),
        compiler_params=params(),
        name="column",
    )(txts, left, right, far)
    left_col, right_col = plane(own_col, 1, 1), plane(own_col, -1, 1)
    onward, across = pl.pallas_call(
        onward_kernel,
        in_specs=[VMEM] * 2,
        out_specs=[VMEM] * 2,
        out_shape=[shape((3 * rows, dt + feat), BF16), shape((2 * rows, dt + feat), BF16)],
        compiler_params=params(),
        cost_estimate=FREE,
        name="onward",
    )(one, two)
    ahead = climb(onward, 2)
    near = swap(across)
    arrays = [shape((images, dt), BF16), shape((images, feat), BF16), shape((images, ds), F32), shape((images, ds), BF16), shape((images, LANES), F32)]
    *arrays_early, self_col, diag, done_early = pl.pallas_call(
        functools.partial(early_kernel, zn, dt),
        in_specs=[SMEM] + [VMEM] * 6,
        out_specs=[VMEM] * 8,
        out_shape=arrays + [shape((images, LANES), F32), shape((rows, ds), F32), shape((8, LANES), F32)],
        scratch_shapes=[pltpu.VMEM((5 * rows, feat), BF16)],
        compiler_params=params(),
        cost_estimate=FREE,
        name="early",
    )(place, proj, st_own, imgs, one, two, near)
    left_col, done_early = together((left_col, done_early))
    far_col = plane(left_col, 1, 1)
    third = swap(ahead[rows:2 * rows])
    timg, feats, simg, simgb, inv = pl.pallas_call(
        functools.partial(late_kernel, zn, dt),
        in_specs=[SMEM] + [VMEM] * 9,
        out_specs=[VMEM] * 5,
        out_shape=arrays,
        scratch_shapes=[pltpu.VMEM((3 * rows, feat), BF16)],
        input_output_aliases={4 + k: k for k in range(5)},
        compiler_params=params(),
        cost_estimate=FREE,
        name="late",
    )(place, proj, ahead, third, *arrays_early, done_early)

    blocks = [(own_col, swap(own_col)), (left_col, swap(left_col)), (right_col, swap(right_col)), None]
    span = column * cn
    stat = self_col
    chain = []
    stats = []
    for n, block in enumerate(blocks):
        final = n == len(blocks) - 1
        if final:
            block = (far_col, swap(far_col))
        big = [shape((images, texts), BF16)] * 3 + [shape((texts, ds), BF16), shape((images, 5 * LANES), F32), shape((images, LANES), F32)]
        out = pl.pallas_call(
            make_block(n, final, gain, [v.shape[0] for v in block]),
            in_specs=[VMEM] * (3 + len(block) + len(chain)),
            out_specs=[VMEM] * (7 if final else 6),
            out_shape=big + ([shape((8, images), F32)] if final else []),
            scratch_shapes=[pltpu.VMEM((images, span), F32)] * 2,
            input_output_aliases={3 + len(block) + k: k for k in range(len(chain))} | ({2: 4} if n else {}),
            compiler_params=params(),
            cost_estimate=FREE,
            name="block" + str(n),
        )(timg, simgb, stat, *block, *chain)
        chain, stat = list(out[:4]), out[4]
        stats.append(out[5])
        if n == 1:
            far_col, stat = together((far_col, stat))
    flat = out[6]
    te, se, sig, stu = chain

    a, c, ft, done_student = pl.pallas_call(
        student_kernel,
        in_specs=[VMEM] * 6,
        out_specs=[VMEM] * 4,
        out_shape=[shape((images, ds), BF16)] * 2 + [shape((feat, images), BF16), shape((8, LANES), F32)],
        compiler_params=params(),
        cost_estimate=FREE,
        name="student",
    )(se, sig, stu, simg, inv, feats)
    b = pl.pallas_call(
        teacher_kernel,
        in_specs=[VMEM] * (4 + len(stats)),
        out_specs=VMEM,
        out_shape=shape((images, ds), BF16),
        scratch_shapes=[pltpu.VMEM((images, texts), BF16)],
        compiler_params=params(),
        cost_estimate=FREE,
        name="teacher",
    )(te, stu, simg, inv, *stats)

    below = lax.ppermute(flat, "z", ring(zn, 1))
    above = lax.ppermute(flat, "z", ring(zn, zn - 1))
    pair, window = pl.pallas_call(
        near_kernel,
        in_specs=[VMEM] * 4,
        out_specs=[VMEM] * 2,
        out_shape=[shape((8, images), F32)] * 2,
        compiler_params=params(),
        name="near",
    )(flat, above, below, done_student)
    ahead = lax.ppermute(window, "z", ring(zn, zn - 3))
    behind = lax.ppermute(pair, "z", ring(zn, 3))

    away, hi, lo, val = pl.pallas_call(
        away_kernel,
        in_specs=[SMEM] + [VMEM] * 9,
        out_specs=[VMEM] * 4,
        out_shape=[shape((half + 8, ds), F32), shape((images, ds), BF16), shape((images, ds), BF16), shape((8, images), F32)],
        scratch_shapes=[pltpu.VMEM((images, LANES), F32), pltpu.VMEM((half, images), BF16)],
        compiler_params=params(),
        cost_estimate=FREE,
        name="away",
    )(place, window, ahead, behind, flat, a, b, c, diag, ft)
    arrived = swap(away)
    home = pl.pallas_call(
        home_kernel,
        in_specs=[SMEM] + [VMEM] * 3,
        out_specs=VMEM,
        out_shape=shape((half, ds), F32),
        scratch_shapes=[pltpu.VMEM((half, images), BF16)],
        compiler_params=params(),
        cost_estimate=FREE,
        name="home",
    )(place, ft, hi, lo)

    cut = half // xn
    keep, *sends = pl.pallas_call(
        functools.partial(cores_kernel, xn),
        in_specs=[SMEM] + [VMEM] * 3,
        out_specs=[VMEM] * 4,
        out_shape=[shape((cut + 8, ds), F32)] + [shape((cut + 16, ds), BF16)] * 3,
        compiler_params=params(),
        name="cores",
    )(place, home, arrived, away)
    got = [lax.ppermute(v, "x", ring(xn, k)) for k, v in zip((1, 3, 2), sends)]
    cut = cut // 2
    mine, across, other = pl.pallas_call(
        rows_kernel,
        in_specs=[SMEM] + [VMEM] * 4,
        out_specs=[VMEM] * 3,
        out_shape=[shape((cut + 8, ds), F32), shape((cut + 16, ds), BF16), shape((cut + 8, ds), F32)],
        scratch_shapes=[pltpu.VMEM((2 * cut, ds), F32)],
        compiler_params=params(),
        name="rows",
    )(place, keep, *got)
    own, loss = pl.pallas_call(
        plane_kernel,
        in_specs=[VMEM] * 4,
        out_specs=[VMEM] * 2,
        out_shape=[shape((cut, ds), F32), shape((8, LANES), F32)],
        compiler_params=params(),
        name="plane",
    )(mine, lax.ppermute(other, Y, ring(yn, 1)), lax.ppermute(other, Y, ring(yn, 3)), lax.ppermute(across, Y, ring(yn, 2)))

    below = lax.ppermute(own, "z", ring(zn, 1))
    above = lax.ppermute(own, "z", ring(zn, zn - 1))
    pair = own + above
    window = pair + below
    ahead = lax.ppermute(window.astype(BF16), "z", ring(zn, zn - 3))
    behind = lax.ppermute(pair.astype(BF16), "z", ring(zn, 3))
    grad = window + ahead.astype(F32) + behind.astype(F32)

    row_loss = lax.dynamic_slice_in_dim(val[0], lax.axis_index("z") * rows, rows, 0)
    return (row_loss, loss[0, 0] / batch, grad)


def solution(mesh):
    sizes = dict(mesh.shape)
    fine = Mesh(np.asarray(mesh.devices).reshape(sizes["blk"] // 2, 2, sizes["img"] // 4, 2, 2), ALL)
    return jax.shard_map(
        per_device,
        mesh=fine,
        in_specs=(P(ALL, None), P(), P(ALL, None), P(ALL, None), P(ALL, None)),
        out_specs=(P(ALL), P(), P(("x", "yl", "c"), None)),
        check_vma=False,
    )
```
